128 devices in a mesh: row: 16 (over x, y), col: 8 (over z, core).
Axes of the slice: x: 4, y: 4, z: 4, core: 2. Of those that a mesh axis runs over, the one named last changes fastest.
Arguments:
- image_student: bfloat16 [16384, 512], P(('row', 'col')), may hold values from -18 to 18
- text_student: bfloat16 [16384, 512], P(('col', 'row')), may hold values from -18 to 18
- image_teacher: bfloat16 [16384, 1280], P(('row', 'col')), may hold values from -18 to 18
- text_teacher: bfloat16 [16384, 1280], P(('col', 'row')), may hold values from -18 to 18
- sketch: bfloat16 [1280, 512], replicated, may hold values from -0.15625 to 0.15625
Outputs:
- grad_image: float32 [16384, 512], P(('row', 'col'))
- grad_text: float32 [16384, 512], P(('col', 'row'))
- mean_loss: float32 [], replicated
The draws below stay inside these ranges and needn't reach their ends.
All inputs are finite; a program needn't handle non-finite values.
Results may differ from the reference program's by a relative error of at most 0.012.
Values may be sent and summed in bfloat16 or wider, within the bound.
No kernel may reach another device: no remote copies, remote signals or barrier semaphores. Data moves between devices by JAX's collectives and lax.ppermute only.
A program may use at most 128 MiB of HBM per device.

```python
import math
import jax
import jax.numpy as jnp
from jax import lax

DS = 512
DT = 1280
ROWS_DEV = 128
PAIRS = 16384
N_ROW = 16
N_COL = 8


def group_strength(key, lowest, highest):
    group_key = jax.random.fold_in(key, 101)
    row_key = jax.random.fold_in(key, 102)
    level = jnp.exp(jax.random.uniform(group_key, (PAIRS // 2, 1), jnp.float32, math.log(lowest), math.log(highest)))
    level = jnp.repeat(level, 2, axis=0)
    jitter = 1.0 + 0.3 * jax.random.uniform(row_key, (PAIRS, 1), jnp.float32)
    return level * jitter


def shared_rows(key, salt, width):
    base = jax.random.truncated_normal(jax.random.fold_in(key, salt), -4.0, 4.0, (PAIRS // 2, width), jnp.float32)
    return jnp.repeat(base, 2, axis=0)


def normal_noise(key, width):
    return jax.random.truncated_normal(jax.random.fold_in(key, 7), -4.0, 4.0, (PAIRS, width), jnp.float32)


def blend(base, noise, strength):
    return ((base + strength * noise) / jnp.sqrt(1.0 + strength * strength)).astype(jnp.bfloat16)


def draw_image_student(key, part):
    strength = group_strength(key, 0.2, 3.0)
    base = shared_rows(key, 201, DS)
    key = jax.random.fold_in(key, 1)
    noise = normal_noise(key, DS)
    return blend(base, noise, strength)


def draw_text_student(key, part):
    strength = group_strength(key, 0.2, 3.0)
    base = shared_rows(key, 201, DS)
    key = jax.random.fold_in(key, 2)
    noise = normal_noise(key, DS)
    return blend(base, noise, strength)


def draw_image_teacher(key, part):
    strength = group_strength(key, 0.2, 3.0)
    base = shared_rows(key, 301, DT)
    key = jax.random.fold_in(key, 3)
    noise = normal_noise(key, DT)
    return blend(base, noise, strength)


def draw_text_teacher(key, part):
    strength = group_strength(key, 0.2, 3.0)
    base = shared_rows(key, 301, DT)
    key = jax.random.fold_in(key, 4)
    noise = normal_noise(key, DT)
    return blend(base, noise, strength)


def centred(stream_key, extent, spread, bound, kind=jnp.bfloat16):
    return jnp.clip(spread * jax.random.normal(stream_key, extent, jnp.float32), -bound, bound).astype(kind)


def setup_inputs(seed: int = 0) -> dict:
    splits = jax.random.split(jax.random.key(seed), 6)
    image_student = draw_image_student(jax.random.fold_in(splits[5], 71), 0)
    text_student = draw_text_student(jax.random.fold_in(splits[5], 71), 0)
    image_teacher = draw_image_teacher(jax.random.fold_in(splits[5], 71), 0)
    text_teacher = draw_text_teacher(jax.random.fold_in(splits[5], 71), 0)
    sketch = centred(splits[4], (DT, DS), DT ** -0.5, 0.15625)
    return {"image_student": image_student, "text_student": text_student, "image_teacher": image_teacher, "text_teacher": text_teacher, "sketch": sketch}


teacher_scale = 100.0
student_scale = 100.0

def unit_rows(x):
    x32 = x.astype(jnp.float32)
    norms = jnp.sqrt(lax.optimization_barrier(jnp.sum(x32 * x32, axis=-1, keepdims=True)) + 1e-06)
    return (x32 / norms, norms)

def reference(image_student, text_student, image_teacher, text_teacher, sketch):
    t_img = unit_rows(jnp.dot(image_teacher, sketch, preferred_element_type=jnp.float32))[0].astype(jnp.bfloat16)
    t_txt = unit_rows(jnp.dot(text_teacher, sketch, preferred_element_type=jnp.float32))[0].astype(jnp.bfloat16)
    u_img, n_img = unit_rows(image_student)
    u_txt, n_txt = unit_rows(text_student)
    s_img = u_img.astype(jnp.bfloat16)
    s_txt = u_txt.astype(jnp.bfloat16)
    block = ROWS_DEV * N_COL
    blocks = N_ROW
    pairs = PAIRS
    t_img_b = t_img.reshape(blocks, block, DS)
    s_img_b = s_img.reshape(blocks, block, DS)

    def tiles(ti, si):
        tea = teacher_scale * jnp.dot(ti, t_txt.T, preferred_element_type=jnp.float32)
        student_logits = student_scale * jnp.dot(si, s_txt.T, preferred_element_type=jnp.float32)
        return (tea, student_logits)

    def column_sweep(carry, input_arrays):
        mp, sp, mq, sq = carry
        tea, student_logits = tiles(input_arrays[0], input_arrays[1])
        nmp = jnp.maximum(mp, lax.optimization_barrier(jnp.max(tea, axis=0)))
        nmq = jnp.maximum(mq, lax.optimization_barrier(jnp.max(student_logits, axis=0)))
        sp = sp * jnp.exp(mp - nmp) + lax.optimization_barrier(jnp.sum(jnp.exp(tea - nmp), axis=0))
        sq = sq * jnp.exp(mq - nmq) + lax.optimization_barrier(jnp.sum(jnp.exp(student_logits - nmq), axis=0))
        return ((nmp, sp, nmq, sq), None)
    low = jnp.full((pairs,), -1e+30, jnp.float32)
    zero = jnp.zeros((pairs,), jnp.float32)
    (cmp_, csp, cmq, csq), _ = lax.scan(column_sweep, (low, zero, low, zero), (t_img_b, s_img_b))
    log_pc_shift = cmp_ + jnp.log(csp)
    log_sc_shift = cmq + jnp.log(csq)

    def grad_pass(carry, input_arrays):
        loss, du_txt = carry
        tea, student_logits = tiles(input_arrays[0], input_arrays[1])
        rmp = lax.optimization_barrier(jnp.max(tea, axis=1, keepdims=True))
        row_max_teacher = lax.optimization_barrier(jnp.max(student_logits, axis=1, keepdims=True))
        log_pr = tea - rmp - jnp.log(lax.optimization_barrier(jnp.sum(jnp.exp(tea - rmp), axis=1, keepdims=True)))
        log_student_row = student_logits - row_max_teacher - jnp.log(lax.optimization_barrier(jnp.sum(jnp.exp(student_logits - row_max_teacher), axis=1, keepdims=True)))
        log_pc = tea - log_pc_shift[None, :]
        log_sc = student_logits - log_sc_shift[None, :]
        pr = jnp.exp(log_pr)
        pc = jnp.exp(log_pc)
        loss = loss + jnp.sum(pr * (log_pr - log_student_row) + pc * (log_pc - log_sc))
        grad = (0.5 * (jnp.exp(log_student_row) - pr + (jnp.exp(log_sc) - pc))).astype(jnp.bfloat16)
        du_img = student_scale * jnp.dot(grad, s_txt, preferred_element_type=jnp.float32)
        du_txt = du_txt + student_scale * jnp.dot(grad.T, input_arrays[1], preferred_element_type=jnp.float32)
        return ((loss, du_txt), du_img)
    init = (jnp.zeros((), jnp.float32), jnp.zeros((pairs, DS), jnp.float32))
    (loss, du_txt), du_img = lax.scan(grad_pass, init, (t_img_b, s_img_b))
    du_img = du_img.reshape(pairs, DS)
    grad_image = (du_img - u_img * lax.optimization_barrier(jnp.sum(u_img * du_img, axis=-1, keepdims=True))) / n_img
    grad_text = (du_txt - u_txt * lax.optimization_barrier(jnp.sum(u_txt * du_txt, axis=-1, keepdims=True))) / n_txt
    mean_loss = 0.5 * loss / pairs
    return (grad_image, grad_text, mean_loss)
```

```python
import math

import jax
import jax.numpy as jnp
from jax import lax
from jax.experimental import pallas as pl
from jax.experimental.pallas import tpu as pltpu
from jax.sharding import PartitionSpec as P

scale = 100.0
LOG2E = math.log2(math.e)
units = scale * LOG2E
SIDE = 4
CORES = 2
AXES = ("row", "col")


def route(step):
    pairs = []
    for x in range(SIDE):
        for y in range(SIDE):
            for z in range(SIDE):
                for k in range(CORES):
                    a, b, c, d = step(x, y, z, k)
                    src = ((x * SIDE + y) * SIDE + z) * CORES + k
                    dst = ((a * SIDE + b) * SIDE + c) * CORES + d
                    pairs.append((src, dst))
    return pairs


def first(e):
    return route(lambda x, y, z, k: (x ^ e, y, z, k) if k == 0 else (x, y ^ e, z, k))


def second(e):
    return route(lambda x, y, z, k: (x, y ^ e, z, k) if k == 0 else (x ^ e, y, z, k))


def along_z(e):
    return route(lambda x, y, z, k: (x, y, z ^ e, k))


def other_core():
    return route(lambda x, y, z, k: (x, y, z, k ^ 1))


def send(x, pairs):
    return lax.ppermute(x, AXES, pairs)


BF16 = jnp.bfloat16
F32 = jnp.float32
NT = (((1,), (1,)), ((), ()))
TN = (((0,), (0,)), ((), ()))
VMEM_LIMIT = 16 * 1024 * 1024
TAIL = 16


def dot(a, b, dims=(((1,), (0,)), ((), ()))):
    return lax.dot_general(a, b, dims, preferred_element_type=F32)


def call(kernel, out_shape, args, flops, exps=0, scratch=(), aliases=None):
    size = sum(a.size * a.dtype.itemsize for a in args)
    size += sum(math.prod(o.shape) * o.dtype.itemsize for o in jax.tree.leaves(out_shape))
    return pl.pallas_call(
        kernel,
        out_shape=out_shape,
        in_specs=[pl.BlockSpec(memory_space=pltpu.VMEM)] * len(args),
        out_specs=jax.tree.map(lambda _: pl.BlockSpec(memory_space=pltpu.VMEM), out_shape),
        scratch_shapes=scratch,
        input_output_aliases=aliases or {},
        compiler_params=pltpu.CompilerParams(vmem_limit_bytes=VMEM_LIMIT),
        cost_estimate=pl.CostEstimate(flops=flops, bytes_accessed=size, transcendentals=exps),
    )(*args)


def unit_rows(x):
    x32 = x.astype(F32)
    norms = jnp.sqrt(jnp.sum(x32 * x32, axis=-1, keepdims=True) + 1e-06)
    return (x32 / norms, norms)


def prepare_kernel(student_ref, teacher_ref, sketch_ref, out_ref):
    width = student_ref.shape[1]
    out_ref[:, :width] = unit_rows(student_ref[...])[0].astype(BF16)
    out_ref[:, width:] = unit_rows(dot(teacher_ref[...], sketch_ref[...]))[0].astype(BF16)


def prepare(student, teacher, sketch):
    rows, width = student.shape
    return call(
        prepare_kernel,
        jax.ShapeDtypeStruct((rows, 2 * width), BF16),
        (student, teacher, sketch),
        2 * rows * sketch.size,
    )


def logits(img, txt, width):
    p = units * dot(img[:, width:], txt[:, width:], NT)
    q = units * dot(img[:, :width], txt[:, :width], NT)
    return p, q


def blocks(img_refs, most=256):
    start = 0
    for ref in img_refs:
        step = min(most, ref.shape[0])
        for at in range(0, ref.shape[0], step):
            yield start + at, ref[at : at + step, :]
        start += ref.shape[0]


def stats_kernel(*refs):
    *img_refs, txt_ref, row_ref, col_ref = refs
    width = txt_ref.shape[1] // 2
    txt = txt_ref[...]
    state = None
    for start, block in blocks(img_refs):
        rows = block.shape[0]
        p, q = logits(block, txt, width)
        d = p - q
        mp = jnp.max(p, axis=1, keepdims=True)
        mq = jnp.max(q, axis=1, keepdims=True)
        e = jnp.exp2(p - mp)
        sp = jnp.sum(e, axis=1, keepdims=True)
        u = jnp.sum(e * d, axis=1, keepdims=True)
        sq = jnp.sum(jnp.exp2(q - mq), axis=1, keepdims=True)
        lane = lax.broadcasted_iota(jnp.int32, (rows, 128), 1)
        packed = jnp.where(lane == 0, mp + jnp.log2(sp), jnp.where(lane == 1, mq + jnp.log2(sq), u / sp))
        for k in range(rows // 128):
            at = start + k * 128
            row_ref[:, at : at + 128] = packed[k * 128 : (k + 1) * 128].T[:8]
        mp = jnp.max(p, axis=0, keepdims=True)
        mq = jnp.max(q, axis=0, keepdims=True)
        if state is not None:
            mp = jnp.maximum(mp, state[0])
            mq = jnp.maximum(mq, state[3])
        e = jnp.exp2(p - mp)
        sp = jnp.sum(e, axis=0, keepdims=True)
        u = jnp.sum(e * d, axis=0, keepdims=True)
        sq = jnp.sum(jnp.exp2(q - mq), axis=0, keepdims=True)
        if state is not None:
            old = jnp.exp2(state[0] - mp)
            sp = sp + old * state[1]
            u = u + old * state[2]
            sq = sq + jnp.exp2(state[3] - mq) * state[4]
        state = (mp, sp, u, mq, sq)
    mp, sp, u, mq, sq = state
    sub = lax.broadcasted_iota(jnp.int32, col_ref.shape, 0)
    col_ref[...] = jnp.where(sub == 0, mp + jnp.log2(sp), jnp.where(sub == 1, mq + jnp.log2(sq), u / sp))


def tile_stats(img, txt):
    rows = sum(i.shape[0] for i in img)
    columns, width = txt.shape
    return call(
        stats_kernel,
        (jax.ShapeDtypeStruct((8, rows), F32), jax.ShapeDtypeStruct((8, columns), F32)),
        (*img, txt),
        2 * rows * columns * width,
        4 * rows * columns,
    )


def merge(parts):
    top = parts[0]
    for part in parts[1:]:
        top = jnp.maximum(top, part)
    weights = [jnp.exp2(part[:2] - top[:2]) for part in parts]
    total = sum(weights)
    lse = top[:2] + jnp.log2(total)
    mean = sum(w[:1] * part[2:] for w, part in zip(weights, parts)) / total[:1]
    return jnp.concatenate([lse, mean], axis=0)


def kl_sum(stats):
    kl = stats[2:3, :] - (stats[0:1, :] - stats[1:2, :])
    return jnp.sum(kl, axis=1, keepdims=True)


def put_tail(ref, at, value):
    shape = (TAIL, ref.shape[1])
    rest = jnp.broadcast_to(value, shape)
    sub = lax.broadcasted_iota(jnp.int32, shape, 0)
    tail = jnp.zeros(shape, F32)
    for n in range(3):
        part = rest.astype(BF16).astype(F32)
        tail = jnp.where(sub == n, part, tail)
        rest = rest - part
    ref[at : at + TAIL, :] = tail.astype(BF16)


def get_tail(ref, at):
    return jnp.sum(ref[at : at + TAIL, :].astype(F32), axis=0, keepdims=True)


def grad_kernel(has_old, last, *refs):
    refs = list(refs)
    g_ref = refs.pop()
    outs = refs[-3:] if last else refs[-2:]
    refs = refs[: -len(outs)]
    all_ref = refs.pop() if last else None
    old_ref = refs.pop() if has_old else None
    *img_refs, txt_ref, row_ref, col_ref = refs
    txt_out = outs[-1]
    columns, width = txt_ref.shape
    width //= 2
    txt = txt_ref[...]
    cp = col_ref[0:1, :] + 1.0
    cq = col_ref[1:2, :] + 1.0
    for start, img in blocks(img_refs):
        rows = img.shape[0]
        span = slice(start, start + rows)
        p, q = logits(img, txt, width)
        turned = []
        for k in range(rows // 128):
            at = start + k * 128
            turned.append(jnp.concatenate([row_ref[:, at : at + 128]] * 16, axis=0).T)
        turned = jnp.concatenate(turned, axis=0) + 1.0
        rp = turned[:, 0:1]
        rq = turned[:, 1:2]
        g = (jnp.exp2(q - rq) - jnp.exp2(p - rp)) + (jnp.exp2(q - cq) - jnp.exp2(p - cp))
        g = g.astype(BF16)
        g_ref[span, :] = g
        part = dot(g, txt[:, :width])
        if has_old:
            part = part + old_ref[span, :]
        if last:
            half = g_ref.shape[0] // 2
            target = outs[0] if start < half else outs[1]
            at = start % half
            target[at : at + rows, :] = part.astype(target.dtype)
        else:
            outs[0][span, :] = part
    total = None
    for start, img in blocks(img_refs, 512):
        part = dot(g_ref[start : start + img.shape[0], :], img[:, :width], TN)
        total = part if total is None else total + part
    txt_out[:columns, :] = total.astype(txt_out.dtype)
    if last:
        put_tail(outs[1], outs[1].shape[0] - TAIL, kl_sum(all_ref[...]))
    else:
        put_tail(txt_out, columns, kl_sum(row_ref[...]))


def tile_grad(img, txt, row, col, old, every=None):
    rows = sum(i.shape[0] for i in img)
    columns, width = txt.shape
    width //= 2
    last = every is not None
    args = [*img, txt, row, col] + [a for a in (old, every) if a is not None]
    shape = jax.ShapeDtypeStruct
    if last:
        out = (shape((rows // 2, width), F32), shape((rows // 2 + TAIL, width), BF16), shape((columns, width), F32))
    else:
        out = (shape((rows, width), F32), shape((columns + TAIL, width), BF16))
    return call(
        lambda *refs: grad_kernel(old is not None, last, *refs),
        out,
        args,
        8 * rows * columns * width,
        4 * rows * columns,
        scratch=[pltpu.VMEM((rows, columns), BF16)],
    )


def combine_kernel(own_ref, stats_ref, *refs):
    count = len(refs) - SIDE
    got, (keep_ref, *out) = refs[:count], refs[count:]
    size = own_ref.shape[0]
    step = size // SIDE
    value = kl_sum(stats_ref[...]) + sum(get_tail(ref, size) for ref in got)
    for n, ref in enumerate([keep_ref, *out]):
        span = slice(n * step, (n + 1) * step)
        total = own_ref[span, :]
        for part in got:
            total = total + part[span, :].astype(F32)
        ref[:step, :] = total.astype(ref.dtype)
        if n:
            put_tail(ref, step, value)
        else:
            ref[step:, :] = jnp.broadcast_to(value, (8, value.shape[1]))


def combine(own, stats, got):
    size, width = own.shape
    step = size // SIDE
    message = jax.ShapeDtypeStruct((step + TAIL, width), BF16)
    keep = jax.ShapeDtypeStruct((step + 8, width), F32)
    return call(combine_kernel, (keep, message, message, message), (own, stats, *got), len(got) * own.size)


def finish_kernel(x_ref, keep_ref, *refs):
    *got, grad_ref, loss_ref = refs
    rows = x_ref.shape[0]
    u, n = unit_rows(x_ref[...])
    du = scale * (keep_ref[:rows, :] + sum(ref[:rows, :].astype(F32) for ref in got))
    grad_ref[...] = (du - u * jnp.sum(u * du, axis=-1, keepdims=True)) / n
    value = keep_ref[rows : rows + 1, :] + sum(get_tail(ref, rows) for ref in got)
    loss_ref[...] = jnp.broadcast_to(value[:, :128], loss_ref.shape)


def finish(x, keep, got):
    out = (jax.ShapeDtypeStruct(x.shape, F32), jax.ShapeDtypeStruct((8, 128), F32))
    return call(finish_kernel, out, (x, keep, *got), 8 * x.size)


def shards(image_student, text_student, image_teacher, text_teacher, sketch):
    rows, width = image_student.shape
    txt = prepare(text_student, text_teacher, sketch)
    img = prepare(image_student, image_teacher, sketch)

    line = jnp.concatenate([txt] + [send(txt, first(e)) for e in range(1, SIDE)], axis=0)
    txt_all = [line] + [send(line, second(e)) for e in range(1, SIDE)]
    img_all = [img] + [send(img, along_z(e)) for e in range(1, SIDE)]
    img_all = img_all + [send(jnp.concatenate(img_all, axis=0), other_core())]

    stats = [tile_stats(img_all, piece) for piece in txt_all]
    row = merge([r[:3] for r, _ in stats]).reshape(3, CORES, SIDE, rows)
    col = jnp.stack([c[:3] for _, c in stats], axis=1).reshape(3, SIDE, SIDE, rows)

    def turn(x, axis, e):
        return jnp.stack([lax.index_in_dim(x, d ^ e, axis, False) for d in range(x.shape[axis])], axis)

    row = merge([row, turn(send(row, other_core()), 1, 1)])
    col = merge([col] + [turn(send(col, second(e)), 1, e) for e in range(1, SIDE)])
    row = merge([row] + [turn(send(row, along_z(e)), 2, e) for e in range(1, SIDE)])
    col = merge([col] + [turn(send(col, first(e)), 2, e) for e in range(1, SIDE)])
    row = row.reshape(3, -1)
    col = col.reshape(3, SIDE, -1)

    row = jnp.pad(row, ((0, 5), (0, 0)))
    col = jnp.pad(col, ((0, 5), (0, 0), (0, 0)))
    old, got = None, []
    for b in range(1, SIDE):
        old, message = tile_grad(img_all, txt_all[b], row, col[:, b], old)
        got.append(send(message, second(b)))
    every = col.reshape(8, -1)
    own_img, message, own_txt = tile_grad(img_all, txt_all[0], row, col[:, 0], old, every)
    keep, *messages = combine(own_img, every, [send(message, other_core())])
    keep_txt, *messages_txt = combine(own_txt, row, got)
    grad_image, col_loss = finish(image_student, keep, [send(m, along_z(e)) for e, m in enumerate(messages, 1)])
    grad_text, row_loss = finish(text_student, keep_txt, [send(m, first(e)) for e, m in enumerate(messages_txt, 1)])
    pairs = rows * lax.axis_size("row") * lax.axis_size("col")
    mean_loss = (0.5 / (LOG2E * pairs)) * (col_loss[0, 0] + row_loss[0, 0])
    return (grad_image, grad_text, mean_loss)


def solution(mesh):
    return jax.shard_map(
        shards,
        mesh=mesh,
        in_specs=(
            P(("row", "col"), None),
            P(("col", "row"), None),
            P(("row", "col"), None),
            P(("col", "row"), None),
            P(),
        ),
        out_specs=(P(("row", "col"), None), P(("col", "row"), None), P()),
        check_vma=False,
    )
```

```python
import math

import jax
import jax.numpy as jnp
from jax import lax
from jax.experimental import pallas as pl
from jax.experimental.pallas import tpu as pltpu
from jax.sharding import PartitionSpec as P

scale = 100.0
LOG2E = math.log2(math.e)
units = scale * LOG2E
SIDE = 4
CORES = 2
AXES = ("row", "col")


def route(step):
    pairs = []
    for x in range(SIDE):
        for y in range(SIDE):
            for z in range(SIDE):
                for k in range(CORES):
                    a, b, c, d = step(x, y, z, k)
                    src = ((x * SIDE + y) * SIDE + z) * CORES + k
                    dst = ((a * SIDE + b) * SIDE + c) * CORES + d
                    pairs.append((src, dst))
    return pairs


def first(e):
    return route(lambda x, y, z, k: (x ^ e, y, z, k) if k == 0 else (x, y ^ e, z, k))


def second(e):
    return route(lambda x, y, z, k: (x, y ^ e, z, k) if k == 0 else (x ^ e, y, z, k))


def along_z(e):
    return route(lambda x, y, z, k: (x, y, z ^ e, k))


def x_or_z(e):
    return route(lambda x, y, z, k: (x ^ e, y, z, k) if k == 0 else (x, y, z ^ e, k))


def along_y(e):
    return route(lambda x, y, z, k: (x, y ^ e, z, k))


def other_core():
    return route(lambda x, y, z, k: (x, y, z, k ^ 1))


def send(x, pairs):
    return lax.ppermute(x, AXES, pairs)


BF16 = jnp.bfloat16
F32 = jnp.float32
NT = (((1,), (1,)), ((), ()))
TN = (((0,), (0,)), ((), ()))
VMEM_LIMIT = 16 * 1024 * 1024
FIRST_LIMIT = 56 * 1024 * 1024
TAIL = 16
BLOCK = 256
SHIFT = 34.0
LOWEST = -60.0


def dot(a, b, dims=(((1,), (0,)), ((), ()))):
    return lax.dot_general(a, b, dims, preferred_element_type=F32)


def call(kernel, out_shape, args, flops=0, scratch=(), hbm=0, limit=VMEM_LIMIT, scalar=None):
    size = sum(a.size * a.dtype.itemsize for a in args)
    size += sum(math.prod(o.shape) * o.dtype.itemsize for o in jax.tree.leaves(out_shape))
    return pl.pallas_call(
        kernel,
        out_shape=out_shape,
        in_specs=[pl.BlockSpec(memory_space=pltpu.HBM)] * hbm + [pl.BlockSpec(memory_space=pltpu.VMEM)] * (len(args) - hbm),
        out_specs=jax.tree.map(
            lambda o: pl.BlockSpec(memory_space=pltpu.SMEM if o is scalar else pltpu.VMEM), out_shape
        ),
        scratch_shapes=scratch,
        compiler_params=pltpu.CompilerParams(vmem_limit_bytes=limit),
        cost_estimate=pl.CostEstimate(flops=flops, bytes_accessed=size, transcendentals=0),
    )(*args)


def unit_rows(x):
    x32 = x.astype(F32)
    norms = jnp.sqrt(jnp.sum(x32 * x32, axis=-1, keepdims=True) + 1e-06)
    return (x32 / norms, norms)


def unit_block(student, teacher, sketch, out_ref):
    width = student.shape[1]
    out_ref[:, :width] = unit_rows(student)[0].astype(BF16)
    out_ref[:, width:] = unit_rows(dot(teacher, sketch))[0].astype(BF16)


def prepare_first_kernel(student_hbm, teacher_hbm, sketch_hbm, out_ref, *refs):
    *buffers, sems = refs
    copies = [
        pltpu.make_async_copy(src, dst, sems.at[n])
        for n, (src, dst) in enumerate(zip((student_hbm, teacher_hbm, sketch_hbm), buffers))
    ]
    for copy in copies:
        copy.start()
    for copy in copies:
        copy.wait()
    unit_block(*(ref[...] for ref in buffers), out_ref)


def prepare_kernel(student_ref, teacher_ref, sketch_ref, out_ref):
    unit_block(student_ref[...], teacher_ref[...], sketch_ref[...], out_ref)


def prepare(student, teacher, sketch, first_kernel):
    rows, width = student.shape
    out = jax.ShapeDtypeStruct((rows, 2 * width), BF16)
    args = (student, teacher, sketch)
    flops = 2 * rows * sketch.size
    if not first_kernel:
        return call(prepare_kernel, out, args, flops)
    scratch = [pltpu.VMEM(x.shape, x.dtype) for x in args] + [pltpu.SemaphoreType.DMA((len(args),))]
    return call(prepare_first_kernel, out, args, flops, scratch, hbm=3, limit=FIRST_LIMIT)


def lay_end_kernel(*refs):
    txt_refs, img_refs, (low_ref, high_ref, img_ref) = refs[:SIDE], refs[SIDE : 2 * SIDE], refs[2 * SIDE :]
    rows = img_refs[0].shape[0]
    for n in range(SIDE):
        img_ref[n * rows : (n + 1) * rows, :] = img_refs[n][...]
        half = low_ref if n < SIDE // 2 else high_ref
        at = n % (SIDE // 2) * rows
        half[at : at + rows, :] = txt_refs[n][...]


def lay_end(txt, img):
    rows, width = txt[0].shape
    half = jax.ShapeDtypeStruct((SIDE // 2 * rows, width), BF16)
    out = (half, half, jax.ShapeDtypeStruct((SIDE * rows, width), BF16))
    return call(lay_end_kernel, out, (*txt, *img))


def products(img, txt_refs):
    width = img.shape[1] // 2
    p = [dot(img[:, width:], ref[:, width:], NT) for ref in txt_refs]
    q = [dot(img[:, :width], ref[:, :width], NT) for ref in txt_refs]
    return jnp.concatenate(p, axis=1), jnp.concatenate(q, axis=1)


def logits(img, txt_refs):
    p, q = products(img, txt_refs)
    return units * p, units * q


def load_block(n, own_ref, other_ref, block_ref):
    half = own_ref.shape[0] // BLOCK

    @pl.when(n < half)
    def _():
        block_ref[...] = own_ref[pl.ds(pl.multiple_of(n * BLOCK, BLOCK), BLOCK), :]

    @pl.when(n >= half)
    def _():
        block_ref[...] = other_ref[pl.ds(pl.multiple_of((n - half) * BLOCK, BLOCK), BLOCK), :]


def put_rows(row_ref, n, first, second, third):
    lane = lax.broadcasted_iota(jnp.int32, (BLOCK, 128), 1)
    packed = jnp.where(lane == 0, first, jnp.where(lane == 1, second, third))
    for k in range(BLOCK // 128):
        at = pl.multiple_of(n * BLOCK + k * 128, 128)
        row_ref[:, pl.ds(at, 128)] = packed[k * 128 : (k + 1) * 128].T[:8]


def stack_rows(first, second, third, shape):
    sub = lax.broadcasted_iota(jnp.int32, shape, 0)
    return jnp.where(sub == 0, first, jnp.where(sub == 1, second, third))


def stats_kernel(has_old, own_ref, other_ref, low_ref, high_ref, *refs):
    txt_refs = (low_ref, high_ref)
    old_ref = refs[0] if has_old else None
    row_ref, col_ref, block_ref = refs[int(has_old) :]
    columns = col_ref.shape[1]
    blocks = 2 * own_ref.shape[0] // BLOCK

    def step(n, state):
        load_block(n, own_ref, other_ref, block_ref)
        p, q = products(block_ref[...], txt_refs)
        ep = jnp.exp2(units * p - SHIFT)
        eq = jnp.exp2(units * q - SHIFT)
        ed = ep * (p - q)
        put_rows(row_ref, n, *(jnp.sum(x, axis=1, keepdims=True) for x in (ep, eq, ed)))
        return tuple(s + jnp.sum(x, axis=0, keepdims=True) for s, x in zip(state, (ep, eq, ed)))

    zero = jnp.zeros((1, columns), F32)
    sp, sq, u = lax.fori_loop(0, blocks, step, (zero, zero, zero))
    rows = row_ref[...]
    lowest = jnp.minimum(jnp.min(rows[0:2, :]), jnp.min(jnp.minimum(sp, sq)))
    col_ref[...] = stack_rows(SHIFT + jnp.log2(sp), SHIFT + jnp.log2(sq), units * u / sp, col_ref.shape)
    row_ref[...] = stack_rows(SHIFT + jnp.log2(rows), SHIFT + jnp.log2(rows), units * rows / rows[0:1], rows.shape)

    @pl.when(lowest < 2.0 ** (LOWEST - SHIFT))
    def _():
        careful_stats(own_ref, other_ref, txt_refs, row_ref, col_ref, block_ref)

    if has_old:
        new, old = row_ref[...], old_ref[...]
        top = jnp.maximum(new, old)
        new_w, old_w = jnp.exp2(new - top), jnp.exp2(old - top)
        total = new_w + old_w
        mean = (new_w[0:1] * new + old_w[0:1] * old) / total[0:1]
        lse = top + jnp.log2(total)
        row_ref[...] = stack_rows(lse, lse, mean, new.shape)


def careful_stats(own_ref, other_ref, txt_refs, row_ref, col_ref, block_ref):
    columns = col_ref.shape[1]

    def step(n, state):
        load_block(n, own_ref, other_ref, block_ref)
        p, q = logits(block_ref[...], txt_refs)
        d = p - q
        mp = jnp.max(p, axis=1, keepdims=True)
        mq = jnp.max(q, axis=1, keepdims=True)
        e = jnp.exp2(p - mp)
        sp = jnp.sum(e, axis=1, keepdims=True)
        u = jnp.sum(e * d, axis=1, keepdims=True)
        sq = jnp.sum(jnp.exp2(q - mq), axis=1, keepdims=True)
        put_rows(row_ref, n, mp + jnp.log2(sp), mq + jnp.log2(sq), u / sp)
        mp = jnp.maximum(jnp.max(p, axis=0, keepdims=True), state[0])
        mq = jnp.maximum(jnp.max(q, axis=0, keepdims=True), state[3])
        e = jnp.exp2(p - mp)
        old = jnp.exp2(state[0] - mp)
        sp = jnp.sum(e, axis=0, keepdims=True) + old * state[1]
        u = jnp.sum(e * d, axis=0, keepdims=True) + old * state[2]
        sq = jnp.sum(jnp.exp2(q - mq), axis=0, keepdims=True) + jnp.exp2(state[3] - mq) * state[4]
        return (mp, sp, u, mq, sq)

    low = jnp.full((1, columns), -1e30, F32)
    zero = jnp.zeros((1, columns), F32)
    blocks = 2 * own_ref.shape[0] // BLOCK
    mp, sp, u, mq, sq = lax.fori_loop(0, blocks, step, (low, zero, zero, low, zero))
    col_ref[...] = stack_rows(mp + jnp.log2(sp), mq + jnp.log2(sq), u / sp, col_ref.shape)


def tile_stats(own, other, txt, old):
    columns = 2 * txt[0].shape[0]
    rows = 2 * own.shape[0]
    args = [own, other, *txt] + ([] if old is None else [old])
    return call(
        lambda *refs: stats_kernel(old is not None, *refs),
        (jax.ShapeDtypeStruct((8, rows), F32), jax.ShapeDtypeStruct((8, columns), F32)),
        args,
        2 * rows * columns * own.shape[1],
        scratch=[pltpu.VMEM((BLOCK, own.shape[1]), BF16)],
    )


def merge(parts):
    top = parts[0]
    for part in parts[1:]:
        top = jnp.maximum(top, part)
    weights = [jnp.exp2(part - top) for part in parts]
    total = sum(weights)
    mean = sum(pltpu.roll(w, 2, 0) * part for w, part in zip(weights, parts)) / pltpu.roll(total, 2, 0)
    sub = lax.broadcasted_iota(jnp.int32, top.shape, 0)
    return jnp.where((sub == 2) | (sub == 5), mean, top + jnp.log2(total))


def on_core(core):
    return pl.when(lax.rem(lax.axis_index("col"), CORES) == core)


def lanes(*index):
    at = 0
    for i in index:
        at = at * SIDE + i
    return slice(at * 128, (at + 1) * 128)


def rows_3(first, second):
    return jnp.concatenate([first[:3], second[:3], first[:2]], axis=0)


def local_kernel(row_ref, c0, c1, c2, c3, out_ref):
    def columns(second, first):
        half, at = divmod(first, SIDE // 2)
        if second in (0, 2):
            return (c0 if second == 0 else c3)[:, lanes(first)]
        return (c1, c2)[half][:, lanes(at + (0 if second == 1 else 2))]

    for core in range(CORES):

        @on_core(core)
        def _():
            for x in range(SIDE):
                for y in range(SIDE):
                    col = columns(y, x) if core == 0 else columns(x, y)
                    row = col
                    if x < CORES:
                        row = row_ref[:, lanes(x if core == 0 else 1 - x, y)]
                    out_ref[:, lanes(x, y)] = rows_3(col, row)


def chip_kernel(own_ref, got_ref, out_ref):
    @on_core(0)
    def _():
        out_ref[...] = rows_3(own_ref[...], got_ref[...])

    @on_core(1)
    def _():
        rows = merge([jnp.concatenate([r[3:6, :1024], r[3:6, :1024], r[:2, :1024]], axis=0) for r in (own_ref, got_ref)])
        out_ref[...] = jnp.zeros(out_ref.shape, F32)
        for z in range(SIDE):
            out_ref[:, lanes(z, 0)] = rows_3(rows[:, lanes(0, z)], rows[:, lanes(1, z)])


def line_kernel(own_ref, g1, g2, g3, out_ref):
    width = own_ref.shape[1] // SIDE
    got = (own_ref, g1, g2, g3)
    for n in range(SIDE):
        parts = [got[e][:, (n ^ e) * width : ((n ^ e) + 1) * width] for e in range(SIDE)]
        out_ref[:, n * width : (n + 1) * width] = merge(parts)


def split_kernel(own_ref, got_ref, col_ref, row_ref):
    for core in range(CORES):

        @on_core(core)
        def _():
            cols, rows = (own_ref, got_ref) if core == 0 else (got_ref, own_ref)
            col_ref[...] = rows_3(cols[3 * core :, :][:3], cols[3 * core :, :][:3])
            for k in range(CORES):
                first = 3 * (k ^ core)
                for z in range(SIDE):
                    part = rows[:, lanes(z, 0)][first : first + 3]
                    row_ref[:, lanes(k, z)] = rows_3(part, part)


def plane_kernel(own_ref, g1, g2, g3, out_ref):
    got = (own_ref, g1, g2, g3)
    for x in range(SIDE):
        for y in range(SIDE):
            part = merge([got[e][:, lanes(x, y ^ e)] for e in range(SIDE)])

            @on_core(0)
            def _():
                out_ref[:, lanes(y, x)] = part

            @on_core(1)
            def _():
                out_ref[:, lanes(x, y)] = part


def exchange(row, cols):
    out = jax.ShapeDtypeStruct((8, len(cols) * cols[0].shape[1]), F32)
    local = call(local_kernel, out, (row, *cols))
    chip = call(chip_kernel, out, (local, send(local, other_core())))
    line = call(line_kernel, out, (chip, *(send(chip, x_or_z(e)) for e in range(1, SIDE))))
    col, row = call(split_kernel, (out, jax.ShapeDtypeStruct(row.shape, F32)), (line, send(line, other_core())))
    return call(plane_kernel, out, (col, *(send(col, along_y(e)) for e in range(1, SIDE)))), row


def kl_sum(stats):
    kl = stats[2:3, :] - (stats[0:1, :] - stats[1:2, :])
    return jnp.sum(kl, axis=1, keepdims=True)


def put_tail(ref, at, value):
    shape = (TAIL, ref.shape[1])
    rest = jnp.broadcast_to(value, shape)
    sub = lax.broadcasted_iota(jnp.int32, shape, 0)
    tail = jnp.zeros(shape, F32)
    for n in range(3):
        part = rest.astype(BF16).astype(F32)
        tail = jnp.where(sub == n, part, tail)
        rest = rest - part
    ref[at : at + TAIL, :] = tail.astype(BF16)


def get_tail(ref, at):
    return jnp.sum(ref[at : at + TAIL, :].astype(F32), axis=0, keepdims=True)


def grad_kernel(piece, own_ref, other_ref, low_ref, high_ref, row_ref, col_ref, *refs):
    txt_refs = (low_ref, high_ref)
    *got, g_ref, out_ref, block_ref = refs
    columns = g_ref.shape[1]
    width = own_ref.shape[1] // 2
    half = own_ref.shape[0]
    blocks = 2 * half // BLOCK
    stats = col_ref[:, piece * columns : (piece + 1) * columns]
    lowest = jnp.minimum(jnp.min(row_ref[0:2, :]), jnp.min(stats[0:2, :]))

    def turned(n, x):
        out = []
        for k in range(BLOCK // 128):
            at = pl.multiple_of(n * BLOCK + k * 128, 128)
            out.append(jnp.concatenate([x(row_ref[:, pl.ds(at, 128)])] * 16, axis=0).T)
        out = jnp.concatenate(out, axis=0)
        return out[:, 0:1], out[:, 1:2]

    @pl.when(lowest >= LOWEST)
    def _():
        col = jnp.exp2(SHIFT - 1.0 - stats)

        def step(n, _):
            load_block(n, own_ref, other_ref, block_ref)
            rp, rq = turned(n, lambda x: jnp.exp2(SHIFT - 1.0 - x))
            p, q = logits(block_ref[...], txt_refs)
            g = jnp.exp2(q - SHIFT) * (rq + col[1:2, :]) - jnp.exp2(p - SHIFT) * (rp + col[0:1, :])
            g_ref[pl.ds(pl.multiple_of(n * BLOCK, BLOCK), BLOCK), :] = g.astype(BF16)
            return 0

        lax.fori_loop(0, blocks, step, 0)

    @pl.when(lowest < LOWEST)
    def _():
        cp = stats[0:1, :] + 1.0
        cq = stats[1:2, :] + 1.0

        def step(n, _):
            load_block(n, own_ref, other_ref, block_ref)
            rp, rq = turned(n, lambda x: x + 1.0)
            p, q = logits(block_ref[...], txt_refs)
            g = (jnp.exp2(q - rq) - jnp.exp2(p - rp)) + (jnp.exp2(q - cq) - jnp.exp2(p - cp))
            g_ref[pl.ds(pl.multiple_of(n * BLOCK, BLOCK), BLOCK), :] = g.astype(BF16)
            return 0

        lax.fori_loop(0, blocks, step, 0)

    total = dot(g_ref[:half, :], own_ref[:, :width], TN) + dot(g_ref[half:, :], other_ref[:, :width], TN)
    if got:
        out_ref[...] = total + got[0][:columns, :].astype(F32)
    else:
        out_ref[:columns, :] = total.astype(BF16)
        put_tail(out_ref, columns, kl_sum(row_ref[...]))


def tile_grad(own, other, txt, row, col, piece, got=None):
    rows = own.shape[0] + other.shape[0]
    columns, width = 2 * txt[0].shape[0], own.shape[1]
    shape = jax.ShapeDtypeStruct
    out = shape((columns + TAIL, width // 2), BF16) if got is None else shape((columns, width // 2), F32)
    return call(
        lambda *refs: grad_kernel(piece, *refs),
        (shape((rows, columns), BF16), out),
        (own, other, *txt, row, col) + (() if got is None else (got,)),
        3 * rows * columns * width,
        scratch=[pltpu.VMEM((BLOCK, width), BF16)],
    )


def image_rows(first, half, grad_refs, txt_refs, store):
    rows, width = txt_refs[0].shape
    width //= 2

    def step(n, _):
        at = pl.multiple_of(n * BLOCK, BLOCK)
        total = None
        for m, txt_ref in enumerate(txt_refs):
            at_column = m % 2 * rows
            part = dot(grad_refs[m // 2][pl.ds(first + at, BLOCK), at_column : at_column + rows], txt_ref[:, :width])
            total = part if total is None else total + part
        store(pl.ds(at, BLOCK), total)
        return 0

    lax.fori_loop(0, half // BLOCK, step, 0)


def other_images_kernel(*refs):
    grad_refs, txt_refs = refs[:SIDE], refs[SIDE : 3 * SIDE]
    stats_ref, own_ref, got_ref, out_ref, sum_ref = refs[3 * SIDE :]
    half = out_ref.shape[0] - TAIL
    sum_ref[...] = own_ref[...] + got_ref[: own_ref.shape[0], :].astype(F32)

    def store(span, value):
        out_ref[span, :] = value.astype(BF16)

    image_rows(half, half, grad_refs, txt_refs, store)
    put_tail(out_ref, half, kl_sum(stats_ref[...]))


def own_images_kernel(*refs):
    grad_refs, txt_refs = refs[:SIDE], refs[SIDE : 3 * SIDE]
    out_ref = refs[-5]
    image_rows(0, out_ref.shape[0], grad_refs, txt_refs, lambda span, value: out_ref.__setitem__((span, slice(None)), value))
    combine_kernel(2, *refs[3 * SIDE : -5], *refs[-4:])


def image_grads(grads, txts, every, row, own, got):
    rows, columns = grads[0].shape
    txts = [half for piece in txts for half in piece]
    width = txts[0].shape[1] // 2
    half = rows // 2
    shape = jax.ShapeDtypeStruct
    flops = half * columns * SIDE * width * 2
    message, own = call(
        other_images_kernel,
        (shape((half + TAIL, width), BF16), shape(own.shape, F32)),
        (*grads, *txts, every, own, got[1]),
        flops,
    )
    step = own.shape[0] // SIDE
    out = shape((step + TAIL, width), BF16)
    own_img, *texts = call(
        own_images_kernel,
        (shape((half, width), F32), shape((step + 8, width), F32), out, out, out),
        (*grads, *txts, own, row, *got),
        flops,
    )
    return message, own_img, texts


def combine_kernel(added, own_ref, stats_ref, *refs):
    count = len(refs) - SIDE
    got, (keep_ref, *out) = refs[:count], refs[count:]
    size = own_ref.shape[0]
    step = size // SIDE
    value = kl_sum(stats_ref[...]) + sum(get_tail(ref, size) for ref in got)
    for n, ref in enumerate([keep_ref, *out]):
        span = slice(n * step, (n + 1) * step)
        total = own_ref[span, :]
        for part in got[added:]:
            total = total + part[span, :].astype(F32)
        ref[:step, :] = total.astype(ref.dtype)
        if n:
            put_tail(ref, step, value)
        else:
            ref[step:, :] = jnp.broadcast_to(value, (8, value.shape[1]))


def combine(own, stats, got):
    size, width = own.shape
    step = size // SIDE
    message = jax.ShapeDtypeStruct((step + TAIL, width), BF16)
    keep = jax.ShapeDtypeStruct((step + 8, width), F32)
    out = (keep, message, message, message)
    return call(lambda *refs: combine_kernel(0, *refs), out, (own, stats, *got))


def tangent(x_ref, keep_ref, got, grad_ref):
    rows = x_ref.shape[0]
    u, n = unit_rows(x_ref[...])
    du = scale * (keep_ref[:rows, :] + sum(ref[:rows, :].astype(F32) for ref in got))
    grad_ref[...] = (du - u * jnp.sum(u * du, axis=-1, keepdims=True)) / n
    return keep_ref[rows : rows + 1, :] + sum(get_tail(ref, rows) for ref in got)


def finish_kernel(factor, *refs):
    *ins, grad_image_ref, grad_text_ref, loss_ref = refs
    each = len(ins) // 2
    value = jnp.zeros((1, grad_text_ref.shape[1]), F32)
    for n, grad_ref in enumerate((grad_image_ref, grad_text_ref)):
        x_ref, keep_ref, *got = ins[n * each : (n + 1) * each]
        value = value + tangent(x_ref, keep_ref, got, grad_ref)
    loss_ref[0, 0] = factor * jnp.max(value)


def finish(image, text, factor):
    loss = jax.ShapeDtypeStruct((1, 1), F32)
    out = tuple(jax.ShapeDtypeStruct(x.shape, F32) for x in (image[0], text[0])) + (loss,)
    return call(lambda *refs: finish_kernel(factor, *refs), out, (*image, *text), scalar=loss)


def shards(image_student, text_student, image_teacher, text_teacher, sketch):
    rows, width = image_student.shape
    txt = prepare(text_student, text_teacher, sketch, True)
    img = prepare(image_student, image_teacher, sketch, False)

    low, high, own = lay_end(
        [txt] + [send(txt, first(e)) for e in range(1, SIDE)],
        [img] + [send(img, along_z(e)) for e in range(1, SIDE)],
    )
    low_1, low_3 = send(low, second(1)), send(low, second(3))
    high_1, high_3 = send(high, second(1)), send(high, second(3))
    low_2, high_2 = send(low_3, second(1)), send(high_1, second(3))
    txt_all = [(low, high), (low_1, high_1), (low_2, high_2), (low_3, high_3)]
    other = send(own, other_core())

    row, cols = None, []
    for pair in ((low, high), (low_1, low_3), (high_1, high_3), (low_2, high_2)):
        row, col = tile_stats(own, other, pair, row)
        cols.append(col)
    col, row = exchange(row, cols)

    grads, got = [None] * SIDE, []
    for b in (2, 1, 3):
        grads[b], message = tile_grad(own, other, txt_all[b], row, col, b)
        got.append(send(message, second(b)))
    grads[0], own_txt = tile_grad(own, other, txt_all[0], row, col, 0, got[0])
    message, own_img, (keep_txt, *messages_txt) = image_grads(grads, txt_all, col, row, own_txt, got)
    keep, *messages = combine(own_img, col, [send(message, other_core())])
    image = [image_student, keep] + [send(m, along_z(e)) for e, m in enumerate(messages, 1)]
    text = [text_student, keep_txt] + [send(m, first(e)) for e, m in enumerate(messages_txt, 1)]
    pairs = rows * lax.axis_size("row") * lax.axis_size("col")
    grad_image, grad_text, mean_loss = finish(image, text, 0.5 / (LOG2E * pairs))
    return (grad_image, grad_text, mean_loss.reshape(()))


def solution(mesh):
    return jax.shard_map(
        shards,
        mesh=mesh,
        in_specs=(
            P(("row", "col"), None),
            P(("col", "row"), None),
            P(("row", "col"), None),
            P(("col", "row"), None),
            P(),
        ),
        out_specs=(P(("row", "col"), None), P(("col", "row"), None), P()),
        check_vma=False,
    )
```

```python
import math

import jax
import jax.numpy as jnp
from jax import lax
from jax.experimental import pallas as pl
from jax.experimental.pallas import tpu as pltpu
from jax.sharding import PartitionSpec as P

scale = 100.0
LOG2E = math.log2(math.e)
units = scale * LOG2E
SIDE = 4
CORES = 2
AXES = ("row", "col")
ORDER = (3, 2, 1)


def route(step):
    pairs = []
    for x in range(SIDE):
        for y in range(SIDE):
            for z in range(SIDE):
                for k in range(CORES):
                    a, b, c, d = step(x, y, z, k)
                    src = ((x * SIDE + y) * SIDE + z) * CORES + k
                    dst = ((a * SIDE + b) * SIDE + c) * CORES + d
                    pairs.append((src, dst))
    return pairs


def first(e):
    return route(lambda x, y, z, k: (x ^ e, y, z, k) if k == 0 else (x, y ^ e, z, k))


def second(e):
    return route(lambda x, y, z, k: (x, y ^ e, z, k) if k == 0 else (x ^ e, y, z, k))


def along_z(e):
    return route(lambda x, y, z, k: (x, y, z ^ e, k))


def x_or_z(e):
    return route(lambda x, y, z, k: (x ^ e, y, z, k) if k == 0 else (x, y, z ^ e, k))


def along_y(e):
    return route(lambda x, y, z, k: (x, y ^ e, z, k))


def other_core():
    return route(lambda x, y, z, k: (x, y, z, k ^ 1))


def send(x, pairs):
    return lax.ppermute(x, AXES, pairs)


BF16 = jnp.bfloat16
F32 = jnp.float32
NT = (((1,), (1,)), ((), ()))
TN = (((0,), (0,)), ((), ()))
VMEM_LIMIT = 16 * 1024 * 1024
FIRST_LIMIT = 56 * 1024 * 1024
TAIL = 16
BLOCK = 256
SHIFT = 34.0
LOWEST = -60.0


def dot(a, b, dims=(((1,), (0,)), ((), ()))):
    return lax.dot_general(a, b, dims, preferred_element_type=F32)


def call(kernel, out_shape, args, flops=0, scratch=(), hbm=0, limit=VMEM_LIMIT):
    size = sum(a.size * a.dtype.itemsize for a in args)
    size += sum(math.prod(o.shape) * o.dtype.itemsize for o in jax.tree.leaves(out_shape))
    return pl.pallas_call(
        kernel,
        out_shape=out_shape,
        in_specs=(
            [pl.BlockSpec(memory_space=pltpu.HBM)] * max(hbm, 0)
            + [pl.BlockSpec(memory_space=pltpu.VMEM)] * (len(args) - abs(hbm))
            + [pl.BlockSpec(memory_space=pl.ANY)] * max(-hbm, 0)
        ),
        out_specs=jax.tree.map(
            lambda o: pl.BlockSpec(memory_space=pltpu.SMEM if o.shape == (1, 1) else pltpu.VMEM), out_shape
        ),
        scratch_shapes=scratch,
        compiler_params=pltpu.CompilerParams(vmem_limit_bytes=limit),
        cost_estimate=pl.CostEstimate(flops=flops, bytes_accessed=size, transcendentals=0),
    )(*args)


def unit_rows(x):
    x32 = x.astype(F32)
    norms = jnp.sqrt(jnp.sum(x32 * x32, axis=-1, keepdims=True) + 1e-06)
    return (x32 / norms, norms)


def unit_block(student, teacher, sketch, out_ref):
    width = student.shape[1]
    out_ref[:, :width] = unit_rows(student)[0].astype(BF16)
    out_ref[:, width:] = unit_rows(dot(teacher, sketch))[0].astype(BF16)


def prepare_first_kernel(student_hbm, teacher_hbm, sketch_hbm, out_ref, *refs):
    *buffers, sems = refs
    copies = [
        pltpu.make_async_copy(src, dst, sems.at[n])
        for n, (src, dst) in enumerate(zip((student_hbm, teacher_hbm, sketch_hbm), buffers))
    ]
    for copy in copies:
        copy.start()
    for copy in copies:
        copy.wait()
    unit_block(*(ref[...] for ref in buffers), out_ref)


def prepare_kernel(student_ref, teacher_ref, sketch_ref, *refs):
    out_ref = refs[-1]
    unit_block(student_ref[...], teacher_ref[...], sketch_ref[...], out_ref)


def prepare(student, teacher, sketch, first_kernel, after=()):
    rows, width = student.shape
    out = jax.ShapeDtypeStruct((rows, 2 * width), BF16)
    args = (student, teacher, sketch)
    flops = 2 * rows * sketch.size
    if not first_kernel:
        return call(prepare_kernel, out, (*args, *after), flops, hbm=-len(after))
    scratch = [pltpu.VMEM(x.shape, x.dtype) for x in args] + [pltpu.SemaphoreType.DMA((len(args),))]
    return call(prepare_first_kernel, out, args, flops, scratch, hbm=3, limit=FIRST_LIMIT)


def lay_end_kernel(count, sizes, *refs):
    blocks = iter(refs[:count])
    for size, out_ref in zip(sizes, refs[count:]):
        at = 0
        for ref in (next(blocks) for _ in range(size)):
            out_ref[at : at + ref.shape[0], :] = ref[...]
            at += ref.shape[0]


def lay_end(groups, after=()):
    width = groups[0][0].shape[1]
    out = [jax.ShapeDtypeStruct((sum(block.shape[0] for block in group), width), BF16) for group in groups]
    args = [block for group in groups for block in group] + list(after)
    sizes = [len(group) for group in groups]
    return call(lambda *refs: lay_end_kernel(len(args), sizes, *refs), out, args, hbm=-len(after))


def products(img, txt_refs):
    width = img.shape[1] // 2
    p = [dot(img[:, width:], ref[:, width:], NT) for ref in txt_refs]
    q = [dot(img[:, :width], ref[:, :width], NT) for ref in txt_refs]
    return jnp.concatenate(p, axis=1), jnp.concatenate(q, axis=1)


def logits(img, txt_refs):
    p, q = products(img, txt_refs)
    return units * p, units * q


def load_block(n, own_ref, other_ref, block_ref):
    half = own_ref.shape[0] // BLOCK

    @pl.when(n < half)
    def _():
        block_ref[...] = own_ref[pl.ds(pl.multiple_of(n * BLOCK, BLOCK), BLOCK), :]

    @pl.when(n >= half)
    def _():
        block_ref[...] = other_ref[pl.ds(pl.multiple_of((n - half) * BLOCK, BLOCK), BLOCK), :]


def put_rows(row_ref, n, first, second, third):
    lane = lax.broadcasted_iota(jnp.int32, (BLOCK, 128), 1)
    packed = jnp.where(lane == 0, first, jnp.where(lane == 1, second, third))
    for k in range(BLOCK // 128):
        at = pl.multiple_of(n * BLOCK + k * 128, 128)
        row_ref[:, pl.ds(at, 128)] = packed[k * 128 : (k + 1) * 128].T[:8]


def put_sums(row_ref, n, *tiles):
    for k in range(BLOCK // 128):
        sums = [jnp.sum(tile[k * 128 : (k + 1) * 128].T, axis=0, keepdims=True) for tile in tiles]
        at = pl.multiple_of(n * BLOCK + k * 128, 128)
        row_ref[:, pl.ds(at, 128)] = stack_rows(*sums, (8, 128))


def stack_rows(first, second, third, shape):
    sub = lax.broadcasted_iota(jnp.int32, shape, 0)
    return jnp.where(sub == 0, first, jnp.where(sub == 1, second, third))


def merge_rows(new, old):
    top = jnp.maximum(new, old)
    new_w, old_w = jnp.exp2(new - top), jnp.exp2(old - top)
    total = new_w + old_w
    mean = (new_w[0:1] * new + old_w[0:1] * old) / total[0:1]
    lse = top + jnp.log2(total)
    return stack_rows(lse, lse, mean, new.shape)


def stats_kernel(pairs, has_old, own_ref, other_ref, *refs):
    halves, refs = refs[: 2 * pairs], refs[2 * pairs :]
    old_ref = refs[0] if has_old else None
    row_ref, col_ref, block_ref, low_ref, high_ref, part_ref = refs[int(has_old) :]
    columns = col_ref.shape[1] // pairs
    blocks = 2 * own_ref.shape[0] // BLOCK

    def step(n, state):
        load_block(n, own_ref, other_ref, block_ref)
        row_sums, out = None, []
        for m in range(pairs):
            p, q = products(block_ref[...], halves[2 * m : 2 * m + 2])
            ep = jnp.exp2(units * p - SHIFT)
            eq = jnp.exp2(units * q - SHIFT)
            tiles = (ep, eq, ep * (p - q))
            out += [s + jnp.sum(x, axis=0, keepdims=True) for s, x in zip(state[3 * m : 3 * m + 3], tiles)]
            part = [sum(x[:, c : c + 128] for c in range(0, columns, 128)) for x in tiles]
            row_sums = part if row_sums is None else [x + y for x, y in zip(row_sums, part)]
        put_sums(row_ref, n, *row_sums)
        return tuple(out)

    zero = jnp.zeros((1, columns), F32)
    state = lax.fori_loop(0, blocks, step, (zero,) * (3 * pairs), unroll=pairs == 1)
    rows = row_ref[...]
    lowest = jnp.min(rows[0:2, :])
    for m in range(pairs):
        sp, sq, u = state[3 * m : 3 * m + 3]
        lowest = jnp.minimum(lowest, jnp.min(jnp.minimum(sp, sq)))
        col_ref[:, m * columns : (m + 1) * columns] = stack_rows(
            SHIFT + jnp.log2(sp), SHIFT + jnp.log2(sq), units * u / sp, (8, columns)
        )
    row_ref[...] = stack_rows(SHIFT + jnp.log2(rows), SHIFT + jnp.log2(rows), units * rows / rows[0:1], rows.shape)

    @pl.when(lowest < 2.0 ** (LOWEST - SHIFT))
    def _():
        def pair(m, _):
            for n in range(pairs):

                @pl.when(m == n)
                def _():
                    low_ref[...] = halves[2 * n][...]
                    high_ref[...] = halves[2 * n + 1][...]

            col = careful_stats(own_ref, other_ref, (low_ref, high_ref), part_ref, columns, block_ref)
            col_ref[:, pl.ds(pl.multiple_of(m * columns, columns), columns)] = col

            @pl.when(m == 0)
            def _():
                row_ref[...] = part_ref[...]

            @pl.when(m > 0)
            def _():
                row_ref[...] = merge_rows(part_ref[...], row_ref[...])

            return 0

        lax.fori_loop(0, pairs, pair, 0)

    if has_old:
        row_ref[...] = merge_rows(row_ref[...], old_ref[...])


def careful_stats(own_ref, other_ref, txt_refs, row_ref, columns, block_ref):

    def step(n, state):
        load_block(n, own_ref, other_ref, block_ref)
        p, q = logits(block_ref[...], txt_refs)
        d = p - q
        mp = jnp.max(p, axis=1, keepdims=True)
        mq = jnp.max(q, axis=1, keepdims=True)
        e = jnp.exp2(p - mp)
        sp = jnp.sum(e, axis=1, keepdims=True)
        u = jnp.sum(e * d, axis=1, keepdims=True)
        sq = jnp.sum(jnp.exp2(q - mq), axis=1, keepdims=True)
        put_rows(row_ref, n, mp + jnp.log2(sp), mq + jnp.log2(sq), u / sp)
        mp = jnp.maximum(jnp.max(p, axis=0, keepdims=True), state[0])
        mq = jnp.maximum(jnp.max(q, axis=0, keepdims=True), state[3])
        e = jnp.exp2(p - mp)
        old = jnp.exp2(state[0] - mp)
        sp = jnp.sum(e, axis=0, keepdims=True) + old * state[1]
        u = jnp.sum(e * d, axis=0, keepdims=True) + old * state[2]
        sq = jnp.sum(jnp.exp2(q - mq), axis=0, keepdims=True) + jnp.exp2(state[3] - mq) * state[4]
        return (mp, sp, u, mq, sq)

    low = jnp.full((1, columns), -1e30, F32)
    zero = jnp.zeros((1, columns), F32)
    blocks = 2 * own_ref.shape[0] // BLOCK
    mp, sp, u, mq, sq = lax.fori_loop(0, blocks, step, (low, zero, zero, low, zero))
    return stack_rows(mp + jnp.log2(sp), mq + jnp.log2(sq), u / sp, (8, columns))


def tile_stats(own, other, halves, old):
    pairs = len(halves) // 2
    half = halves[0].shape
    columns = len(halves) * half[0]
    rows = 2 * own.shape[0]
    args = [own, other, *halves] + ([] if old is None else [old])
    return call(
        lambda *refs: stats_kernel(pairs, old is not None, *refs),
        (jax.ShapeDtypeStruct((8, rows), F32), jax.ShapeDtypeStruct((8, columns), F32)),
        args,
        2 * rows * columns * own.shape[1],
        scratch=[
            pltpu.VMEM((BLOCK, half[1]), BF16),
            pltpu.VMEM(half, BF16),
            pltpu.VMEM(half, BF16),
            pltpu.VMEM((8, rows), F32),
        ],
    )


def merge(parts):
    top = parts[0]
    for part in parts[1:]:
        top = jnp.maximum(top, part)
    weights = [jnp.exp2(part - top) for part in parts]
    total = sum(weights)
    mean = sum(pltpu.roll(w, 2, 0) * part for w, part in zip(weights, parts)) / pltpu.roll(total, 2, 0)
    sub = lax.broadcasted_iota(jnp.int32, top.shape, 0)
    return jnp.where((sub == 2) | (sub == 5), mean, top + jnp.log2(total))


def on_core(core):
    return pl.when(lax.rem(lax.axis_index("col"), CORES) == core)


def lanes(*index):
    at = 0
    for i in index:
        at = at * SIDE + i
    return slice(at * 128, (at + 1) * 128)


def rows_3(first, second):
    return jnp.concatenate([first[:3], second[:3], first[:2]], axis=0)


def local_kernel(row_ref, near_ref, far_ref, out_ref):
    def columns(second, first):
        if second == 2:
            return far_ref[:, lanes(first)]
        half, at = divmod(first, SIDE // 2)
        return near_ref[:, lanes({0: (0, 2), 1: (4, 8), 3: (6, 10)}[second][half] + at)]

    for core in range(CORES):

        @on_core(core)
        def _():
            for x in range(SIDE):
                for y in range(SIDE):
                    col = columns(y, x) if core == 0 else columns(x, y)
                    row = col
                    if x < CORES:
                        row = row_ref[:, lanes(x if core == 0 else 1 - x, y)]
                    out_ref[:, lanes(x, y)] = rows_3(col, row)


def chip_kernel(own_ref, got_ref, out_ref):
    @on_core(0)
    def _():
        out_ref[...] = rows_3(own_ref[...], got_ref[...])

    @on_core(1)
    def _():
        rows = merge([jnp.concatenate([r[3:6, :1024], r[3:6, :1024], r[:2, :1024]], axis=0) for r in (own_ref, got_ref)])
        out_ref[...] = jnp.zeros(out_ref.shape, F32)
        for z in range(SIDE):
            out_ref[:, lanes(z, 0)] = rows_3(rows[:, lanes(0, z)], rows[:, lanes(1, z)])


def line_kernel(own_ref, g3, g2, g1, out_ref):
    width = own_ref.shape[1] // SIDE
    got = (own_ref, g1, g2, g3)
    for n in range(SIDE):
        parts = [got[e][:, (n ^ e) * width : ((n ^ e) + 1) * width] for e in range(SIDE)]
        out_ref[:, n * width : (n + 1) * width] = merge(parts)


def split_kernel(own_ref, got_ref, col_ref, row_ref):
    for core in range(CORES):

        @on_core(core)
        def _():
            cols, rows = (own_ref, got_ref) if core == 0 else (got_ref, own_ref)
            col_ref[...] = rows_3(cols[3 * core :, :][:3], cols[3 * core :, :][:3])
            for k in range(CORES):
                first = 3 * (k ^ core)
                for z in range(SIDE):
                    part = rows[:, lanes(z, 0)][first : first + 3]
                    row_ref[:, lanes(k, z)] = rows_3(part, part)


def plane_kernel(own_ref, g3, g2, g1, row_ref, out_ref, row_tail_ref, col_tail_ref, lowest_ref):
    got = (own_ref, g1, g2, g3)
    for x in range(SIDE):
        for y in range(SIDE):
            part = merge([got[e][:, lanes(x, y ^ e)] for e in range(SIDE)])

            @on_core(0)
            def _():
                out_ref[:, lanes(y, x)] = part

            @on_core(1)
            def _():
                out_ref[:, lanes(x, y)] = part

    put_tail(row_tail_ref, 0, kl_sum(row_ref[...]))
    put_tail(col_tail_ref, 0, kl_sum(out_ref[...]))
    lowest = jnp.minimum(
        jnp.min(row_ref[0:2, :], axis=1, keepdims=True), jnp.min(out_ref[0:2, :], axis=1, keepdims=True)
    )
    lowest_ref[...] = jnp.broadcast_to(jnp.min(lowest, axis=0, keepdims=True), lowest_ref.shape)


def exchange(row, cols):
    columns = sum(col.shape[1] for col in cols)
    out = jax.ShapeDtypeStruct((8, columns), F32)
    tail = jax.ShapeDtypeStruct((TAIL, columns // SIDE), BF16)
    local = call(local_kernel, out, (row, *cols))
    chip = call(chip_kernel, out, (local, send(local, other_core())))
    line = call(line_kernel, out, (chip, *(send(chip, x_or_z(e)) for e in ORDER)))
    col, row = call(split_kernel, (out, jax.ShapeDtypeStruct(row.shape, F32)), (line, send(line, other_core())))
    parts = [send(col, along_y(e)) for e in ORDER]
    col, *rest = call(plane_kernel, (out, tail, tail, jax.ShapeDtypeStruct((8, 128), F32)), (col, *parts, row))
    return row, col, *rest


def kl_sum(stats):
    kl = stats[2:3, :] - (stats[0:1, :] - stats[1:2, :])
    return jnp.sum(kl, axis=1, keepdims=True)


def put_tail(ref, at, value):
    shape = (TAIL, ref.shape[1])
    rest = jnp.broadcast_to(value, shape)
    sub = lax.broadcasted_iota(jnp.int32, shape, 0)
    tail = jnp.zeros(shape, F32)
    for n in range(3):
        part = rest.astype(BF16).astype(F32)
        tail = jnp.where(sub == n, part, tail)
        rest = rest - part
    ref[at : at + TAIL, :] = tail.astype(BF16)


def get_tail(ref, at):
    return jnp.sum(ref[at : at + TAIL, :].astype(F32), axis=0, keepdims=True)


def grad_kernel(piece, own_ref, other_ref, low_ref, high_ref, row_ref, col_ref, lowest_ref, *refs):
    *tail, g_ref, out_ref, block_ref = refs
    txt_refs = (low_ref, high_ref)
    columns = g_ref.shape[1]
    width = own_ref.shape[1] // 2
    half = own_ref.shape[0]
    blocks = 2 * half // BLOCK
    stats = col_ref[:, piece * columns : (piece + 1) * columns]
    lowest = lowest_ref[0, 0]

    def turned(n, x):
        out = []
        for k in range(BLOCK // 128):
            at = pl.multiple_of(n * BLOCK + k * 128, 128)
            out.append(jnp.concatenate([x(row_ref[:, pl.ds(at, 128)])] * 16, axis=0).T)
        out = jnp.concatenate(out, axis=0)
        return out[:, 0:1], out[:, 1:2]

    @pl.when(lowest >= LOWEST)
    def _():
        col = jnp.exp2(SHIFT - 1.0 - stats)

        def step(n, _):
            load_block(n, own_ref, other_ref, block_ref)
            rp, rq = turned(n, lambda x: jnp.exp2(SHIFT - 1.0 - x))
            p, q = logits(block_ref[...], txt_refs)
            g = jnp.exp2(q - SHIFT) * (rq + col[1:2, :]) - jnp.exp2(p - SHIFT) * (rp + col[0:1, :])
            g_ref[pl.ds(pl.multiple_of(n * BLOCK, BLOCK), BLOCK), :] = g.astype(BF16)
            return 0

        lax.fori_loop(0, blocks, step, 0, unroll=True)

    @pl.when(lowest < LOWEST)
    def _():
        cp = stats[0:1, :] + 1.0
        cq = stats[1:2, :] + 1.0

        def step(n, _):
            load_block(n, own_ref, other_ref, block_ref)
            rp, rq = turned(n, lambda x: x + 1.0)
            p, q = logits(block_ref[...], txt_refs)
            g = (jnp.exp2(q - rq) - jnp.exp2(p - rp)) + (jnp.exp2(q - cq) - jnp.exp2(p - cp))
            g_ref[pl.ds(pl.multiple_of(n * BLOCK, BLOCK), BLOCK), :] = g.astype(BF16)
            return 0

        lax.fori_loop(0, blocks, step, 0)

    total = dot(g_ref[:half, :], own_ref[:, :width], TN) + dot(g_ref[half:, :], other_ref[:, :width], TN)
    out_ref[:columns, :] = total.astype(out_ref.dtype)
    if tail:
        out_ref[columns:, :] = tail[0][...]


def tile_grad(own, other, txt, stats, piece):
    row, col, row_tail, _, lowest = stats
    rows = own.shape[0] + other.shape[0]
    columns, width = 2 * txt[0].shape[0], own.shape[1]
    shape = jax.ShapeDtypeStruct
    out = shape((columns + TAIL, width // 2), BF16) if piece else shape((columns, width // 2), F32)
    return call(
        lambda *refs: grad_kernel(piece, *refs),
        (shape((rows, columns), BF16), out),
        (own, other, *txt, row, col, lowest) + ((row_tail,) if piece else ()),
        3 * rows * columns * width,
        scratch=[pltpu.VMEM((BLOCK, width), BF16)],
    )


def image_rows(first, half, grad_refs, txt_refs, store):
    rows, width = txt_refs[0].shape
    width //= 2

    def step(n, _):
        at = pl.multiple_of(n * BLOCK, BLOCK)
        total = None
        for m, txt_ref in enumerate(txt_refs):
            at_column = m % 2 * rows
            part = dot(grad_refs[m // 2][pl.ds(first + at, BLOCK), at_column : at_column + rows], txt_ref[:, :width])
            total = part if total is None else total + part
        store(pl.ds(at, BLOCK), total)
        return 0

    lax.fori_loop(0, half // BLOCK, step, 0, unroll=True)


def other_images_kernel(*refs):
    tail_ref, out_ref = refs[3 * SIDE :]
    half = out_ref.shape[0] - TAIL

    def store(span, value):
        out_ref[span, :] = value.astype(BF16)

    image_rows(half, half, refs[:SIDE], refs[SIDE : 3 * SIDE], store)
    out_ref[half:, :] = tail_ref[...]


def own_images_kernel(*refs):
    out_ref = refs[-5]

    def store(span, value):
        out_ref[span, :] = value

    image_rows(0, out_ref.shape[0], refs[:SIDE], refs[SIDE : 3 * SIDE], store)
    combine_kernel(*refs[3 * SIDE : -5], *refs[-4:])


def image_grads(grads, txts, stats, own, got):
    rows, columns = grads[0].shape
    txts = [half for piece in txts for half in piece]
    width = txts[0].shape[1] // 2
    half = rows // 2
    shape = jax.ShapeDtypeStruct
    flops = half * columns * SIDE * width * 2
    message = call(other_images_kernel, shape((half + TAIL, width), BF16), (*grads, *txts, stats[3]), flops)
    step = own.shape[0] // SIDE
    out = shape((step + TAIL, width), BF16)
    own_img, *texts = call(
        own_images_kernel,
        (shape((half, width), F32), shape((step + 8, width), F32), out, out, out),
        (*grads, *txts, own, stats[2], *got),
        flops,
    )
    return message, own_img, texts


def combine_kernel(own_ref, tail_ref, *refs):
    count = len(refs) - SIDE
    got, outs = refs[:count], refs[count:]
    size = own_ref.shape[0]
    step = size // SIDE
    value = get_tail(tail_ref, 0) + sum(get_tail(ref, size) for ref in got)
    for n, ref in enumerate(outs):
        span = slice(n * step, (n + 1) * step)
        total = own_ref[span, :]
        for part in got:
            total = total + part[span, :].astype(F32)
        ref[:step, :] = total.astype(ref.dtype)
        if n:
            put_tail(ref, step, value)
        else:
            ref[step:, :] = jnp.broadcast_to(value, (8, value.shape[1]))


def combine(own, tail, got):
    size, width = own.shape
    step = size // SIDE
    message = jax.ShapeDtypeStruct((step + TAIL, width), BF16)
    keep = jax.ShapeDtypeStruct((step + 8, width), F32)
    return call(combine_kernel, (keep, message, message, message), (own, tail, *got))


def tangent(x_ref, keep_ref, got, grad_ref):
    rows = x_ref.shape[0]
    u, n = unit_rows(x_ref[...])
    du = scale * (keep_ref[:rows, :] + sum(ref[:rows, :].astype(F32) for ref in got))
    grad_ref[...] = (du - u * jnp.sum(u * du, axis=-1, keepdims=True)) / n
    return keep_ref[rows : rows + 1, :] + sum(get_tail(ref, rows) for ref in got)


def finish_kernel(factor, *refs):
    *ins, grad_image_ref, grad_text_ref, loss_ref = refs
    each = len(ins) // 2
    value = jnp.zeros((1, grad_text_ref.shape[1]), F32)
    for n, grad_ref in enumerate((grad_image_ref, grad_text_ref)):
        x_ref, keep_ref, *got = ins[n * each : (n + 1) * each]
        value = value + tangent(x_ref, keep_ref, got, grad_ref)
    loss_ref[0, 0] = factor * jnp.max(value)


def finish(image, text, factor):
    loss = jax.ShapeDtypeStruct((1, 1), F32)
    out = tuple(jax.ShapeDtypeStruct(x.shape, F32) for x in (image[0], text[0])) + (loss,)
    return call(lambda *refs: finish_kernel(factor, *refs), out, (*image, *text))


def shards(image_student, text_student, image_teacher, text_teacher, sketch):
    rows, width = image_student.shape
    txt = prepare(text_student, text_teacher, sketch, True)

    blocks = [txt] + [send(txt, first(e)) for e in range(1, SIDE)]
    img = prepare(image_student, image_teacher, sketch, False, (blocks[1],))
    img_1, img_3 = send(img, along_z(1)), send(img, along_z(3))
    low, high = lay_end([blocks[:2], blocks[2:]], (img_1, img_3))
    low_1, low_3 = send(low, second(1)), send(low, second(3))
    high_1, high_3 = send(high, second(1)), send(high, second(3))
    low_2, high_2 = send(low_3, second(1)), send(high_1, second(3))
    txt_all = [(low, high), (low_1, high_1), (low_2, high_2), (low_3, high_3)]
    (own,) = lay_end([[img, img_1, send(img, along_z(2)), img_3]], (low_1, low_3, high_1, high_3))
    other = send(own, other_core())

    row, near_col = tile_stats(own, other, (low, high, low_1, low_3, high_1, high_3), None)
    row, far_col = tile_stats(own, other, (low_2, high_2), row)
    stats = exchange(row, (near_col, far_col))

    grads, got = [None] * SIDE, []
    for b in (2, 1, 3):
        grads[b], message = tile_grad(own, other, txt_all[b], stats, b)
        got.append(send(message, second(b)))
    grads[0], own_txt = tile_grad(own, other, txt_all[0], stats, 0)
    message, own_img, (keep_txt, *messages_txt) = image_grads(grads, txt_all, stats, own_txt, got)
    keep, *messages = combine(own_img, stats[3], [send(message, other_core())])
    image = [image_student, keep] + [send(messages[e - 1], along_z(e)) for e in (3, 2, 1)]
    text = [text_student, keep_txt] + [send(messages_txt[e - 1], first(e)) for e in (3, 2, 1)]
    pairs = rows * lax.axis_size("row") * lax.axis_size("col")
    grad_image, grad_text, mean_loss = finish(image, text, 0.5 / (LOG2E * pairs))
    return (grad_image, grad_text, mean_loss.reshape(()))


def solution(mesh):
    return jax.shard_map(
        shards,
        mesh=mesh,
        in_specs=(
            P(("row", "col"), None),
            P(("col", "row"), None),
            P(("row", "col"), None),
            P(("col", "row"), None),
            P(),
        ),
        out_specs=(P(("row", "col"), None), P(("col", "row"), None), P()),
        check_vma=False,
    )
```

```python
import math

import jax
import jax.numpy as jnp
from jax import lax
from jax.experimental import pallas as pl
from jax.experimental.pallas import tpu as pltpu
from jax.sharding import PartitionSpec as P

scale = 100.0
LOG2E = math.log2(math.e)
units = scale * LOG2E
SIDE = 4
CORES = 2
AXES = ("row", "col")
ORDER = (1, 2, 3)


def route(step):
    pairs = []
    for x in range(SIDE):
        for y in range(SIDE):
            for z in range(SIDE):
                for k in range(CORES):
                    a, b, c, d = step(x, y, z, k)
                    src = ((x * SIDE + y) * SIDE + z) * CORES + k
                    dst = ((a * SIDE + b) * SIDE + c) * CORES + d
                    pairs.append((src, dst))
    return pairs


def first(e):
    return route(lambda x, y, z, k: (x ^ e, y, z, k) if k == 0 else (x, y ^ e, z, k))


def second(e):
    return route(lambda x, y, z, k: (x, y ^ e, z, k) if k == 0 else (x ^ e, y, z, k))


def along_z(e):
    return route(lambda x, y, z, k: (x, y, z ^ e, k))


def x_or_z(e):
    return route(lambda x, y, z, k: (x ^ e, y, z, k) if k == 0 else (x, y, z ^ e, k))


def along_y(e):
    return route(lambda x, y, z, k: (x, y ^ e, z, k))


def other_core():
    return route(lambda x, y, z, k: (x, y, z, k ^ 1))


def send(x, pairs):
    return lax.ppermute(x, AXES, pairs)


BF16 = jnp.bfloat16
F32 = jnp.float32
NT = (((1,), (1,)), ((), ()))
TN = (((0,), (0,)), ((), ()))
VMEM_LIMIT = 16 * 1024 * 1024
FIRST_LIMIT = 56 * 1024 * 1024
TAIL = 16
BLOCK = 256
SHIFT = 34.0
LOWEST = -60.0


def dot(a, b, dims=(((1,), (0,)), ((), ()))):
    return lax.dot_general(a, b, dims, preferred_element_type=F32)


def call(kernel, out_shape, args, flops=0, scratch=(), hbm=0, limit=VMEM_LIMIT):
    size = sum(a.size * a.dtype.itemsize for a in args)
    size += sum(math.prod(o.shape) * o.dtype.itemsize for o in jax.tree.leaves(out_shape))
    size = size if flops else 0
    return pl.pallas_call(
        kernel,
        out_shape=out_shape,
        in_specs=(
            [pl.BlockSpec(memory_space=pltpu.HBM)] * max(hbm, 0)
            + [pl.BlockSpec(memory_space=pltpu.VMEM)] * (len(args) - abs(hbm))
            + [pl.BlockSpec(memory_space=pl.ANY)] * max(-hbm, 0)
        ),
        out_specs=jax.tree.map(
            lambda o: pl.BlockSpec(memory_space=pltpu.SMEM if o.shape == (1, 1) else pltpu.VMEM), out_shape
        ),
        scratch_shapes=scratch,
        compiler_params=pltpu.CompilerParams(vmem_limit_bytes=limit),
        cost_estimate=pl.CostEstimate(flops=flops, bytes_accessed=size, transcendentals=0),
    )(*args)


def unit_rows(x):
    x32 = x.astype(F32)
    norms = jnp.sqrt(jnp.sum(x32 * x32, axis=-1, keepdims=True) + 1e-06)
    return (x32 / norms, norms)


def unit_block(student, teacher, sketch, out_ref):
    width = student.shape[1]
    out_ref[:, :width] = unit_rows(student)[0].astype(BF16)
    out_ref[:, width:] = unit_rows(dot(teacher, sketch))[0].astype(BF16)


def prepare_first_kernel(student_hbm, teacher_hbm, sketch_hbm, out_ref, *refs):
    *buffers, sems = refs
    copies = [
        pltpu.make_async_copy(src, dst, sems.at[n])
        for n, (src, dst) in enumerate(zip((student_hbm, teacher_hbm, sketch_hbm), buffers))
    ]
    for copy in copies:
        copy.start()
    for copy in copies:
        copy.wait()
    unit_block(*(ref[...] for ref in buffers), out_ref)


def prepare_kernel(student_ref, teacher_ref, sketch_ref, *refs):
    out_ref = refs[-1]
    unit_block(student_ref[...], teacher_ref[...], sketch_ref[...], out_ref)


def prepare(student, teacher, sketch, first_kernel, after=()):
    rows, width = student.shape
    out = jax.ShapeDtypeStruct((rows, 2 * width), BF16)
    args = (student, teacher, sketch)
    flops = 2 * rows * sketch.size
    if not first_kernel:
        return call(prepare_kernel, out, (*args, *after), flops, hbm=-len(after))
    scratch = [pltpu.VMEM(x.shape, x.dtype) for x in args] + [pltpu.SemaphoreType.DMA((len(args),))]
    return call(prepare_first_kernel, out, args, flops, scratch, hbm=3, limit=FIRST_LIMIT)


def lay_end_kernel(count, sizes, *refs):
    blocks = iter(refs[:count])
    for size, out_ref in zip(sizes, refs[count:]):
        at = 0
        for ref in (next(blocks) for _ in range(size)):
            out_ref[at : at + ref.shape[0], :] = ref[...]
            at += ref.shape[0]


def lay_end(groups, after=()):
    width = groups[0][0].shape[1]
    out = [jax.ShapeDtypeStruct((sum(block.shape[0] for block in group), width), BF16) for group in groups]
    args = [block for group in groups for block in group] + list(after)
    sizes = [len(group) for group in groups]
    return call(lambda *refs: lay_end_kernel(len(args), sizes, *refs), out, args, hbm=-len(after))


def products(img, txt_refs):
    width = img.shape[1] // 2
    p = [dot(img[:, width:], ref[:, width:], NT) for ref in txt_refs]
    q = [dot(img[:, :width], ref[:, :width], NT) for ref in txt_refs]
    return jnp.concatenate(p, axis=1), jnp.concatenate(q, axis=1)


def logits(img, txt_refs):
    p, q = products(img, txt_refs)
    return units * p, units * q


def load_block(n, own_ref, other_ref, block_ref):
    half = own_ref.shape[0] // BLOCK

    @pl.when(n < half)
    def _():
        block_ref[...] = own_ref[pl.ds(pl.multiple_of(n * BLOCK, BLOCK), BLOCK), :]

    @pl.when(n >= half)
    def _():
        block_ref[...] = other_ref[pl.ds(pl.multiple_of((n - half) * BLOCK, BLOCK), BLOCK), :]


def put_rows(row_ref, n, first, second, third):
    lane = lax.broadcasted_iota(jnp.int32, (BLOCK, 128), 1)
    packed = jnp.where(lane == 0, first, jnp.where(lane == 1, second, third))
    for k in range(BLOCK // 128):
        at = pl.multiple_of(n * BLOCK + k * 128, 128)
        row_ref[:, pl.ds(at, 128)] = packed[k * 128 : (k + 1) * 128].T[:8]


def put_sums(row_ref, n, *tiles):
    for k in range(BLOCK // 128):
        sums = [jnp.sum(tile[k * 128 : (k + 1) * 128].T, axis=0, keepdims=True) for tile in tiles]
        at = pl.multiple_of(n * BLOCK + k * 128, 128)
        row_ref[:, pl.ds(at, 128)] = stack_rows(*sums, (8, 128))


def stack_rows(first, second, third, shape):
    sub = lax.broadcasted_iota(jnp.int32, shape, 0)
    return jnp.where(sub == 0, first, jnp.where(sub == 1, second, third))


def merge_rows(new, old):
    top = jnp.maximum(new, old)
    new_w, old_w = jnp.exp2(new - top), jnp.exp2(old - top)
    total = new_w + old_w
    mean = (new_w[0:1] * new + old_w[0:1] * old) / total[0:1]
    lse = top + jnp.log2(total)
    return stack_rows(lse, lse, mean, new.shape)


def stats_kernel(pairs, has_old, own_ref, other_ref, *refs):
    halves, refs = refs[: 2 * pairs], refs[2 * pairs :]
    old_ref = refs[0] if has_old else None
    row_ref, col_ref, *tile_refs, block_ref, low_ref, high_ref, part_ref = refs[int(has_old) :]
    columns = col_ref.shape[1] // pairs
    blocks = 2 * own_ref.shape[0] // BLOCK

    def step(n, state):
        load_block(n, own_ref, other_ref, block_ref)
        row_sums, out = None, []
        for m in range(pairs):
            p, q = products(block_ref[...], halves[2 * m : 2 * m + 2])
            ep = jnp.exp2(units * p - SHIFT)
            eq = jnp.exp2(units * q - SHIFT)
            tiles = (ep, eq, ep * (p - q))
            span = pl.ds(pl.multiple_of(n * BLOCK, BLOCK), BLOCK)
            for k in range(4):
                at = k // 2 * (columns // 2)
                tile_refs[4 * m + k][span, :] = tiles[k % 2][:, at : at + columns // 2]
            out += [s + jnp.sum(x, axis=0, keepdims=True) for s, x in zip(state[3 * m : 3 * m + 3], tiles)]
            part = [sum(x[:, c : c + 128] for c in range(0, columns, 128)) for x in tiles]
            row_sums = part if row_sums is None else [x + y for x, y in zip(row_sums, part)]
        put_sums(row_ref, n, *row_sums)
        return tuple(out)

    zero = jnp.zeros((1, columns), F32)
    state = lax.fori_loop(0, blocks, step, (zero,) * (3 * pairs), unroll=pairs == 1)
    rows = row_ref[...]
    lowest = jnp.min(rows[0:2, :])
    for m in range(pairs):
        sp, sq, u = state[3 * m : 3 * m + 3]
        lowest = jnp.minimum(lowest, jnp.min(jnp.minimum(sp, sq)))
        col_ref[:, m * columns : (m + 1) * columns] = stack_rows(
            SHIFT + jnp.log2(sp), SHIFT + jnp.log2(sq), units * u / sp, (8, columns)
        )
    row_ref[...] = stack_rows(SHIFT + jnp.log2(rows), SHIFT + jnp.log2(rows), units * rows / rows[0:1], rows.shape)

    @pl.when(lowest < 2.0 ** (LOWEST - SHIFT))
    def _():
        def pair(m, _):
            for n in range(pairs):

                @pl.when(m == n)
                def _():
                    low_ref[...] = halves[2 * n][...]
                    high_ref[...] = halves[2 * n + 1][...]

            col = careful_stats(own_ref, other_ref, (low_ref, high_ref), part_ref, columns, block_ref)
            col_ref[:, pl.ds(pl.multiple_of(m * columns, columns), columns)] = col

            @pl.when(m == 0)
            def _():
                row_ref[...] = part_ref[...]

            @pl.when(m > 0)
            def _():
                row_ref[...] = merge_rows(part_ref[...], row_ref[...])

            return 0

        lax.fori_loop(0, pairs, pair, 0)

    if has_old:
        row_ref[...] = merge_rows(row_ref[...], old_ref[...])


def careful_stats(own_ref, other_ref, txt_refs, row_ref, columns, block_ref):

    def step(n, state):
        load_block(n, own_ref, other_ref, block_ref)
        p, q = logits(block_ref[...], txt_refs)
        d = p - q
        mp = jnp.max(p, axis=1, keepdims=True)
        mq = jnp.max(q, axis=1, keepdims=True)
        e = jnp.exp2(p - mp)
        sp = jnp.sum(e, axis=1, keepdims=True)
        u = jnp.sum(e * d, axis=1, keepdims=True)
        sq = jnp.sum(jnp.exp2(q - mq), axis=1, keepdims=True)
        put_rows(row_ref, n, mp + jnp.log2(sp), mq + jnp.log2(sq), u / sp)
        mp = jnp.maximum(jnp.max(p, axis=0, keepdims=True), state[0])
        mq = jnp.maximum(jnp.max(q, axis=0, keepdims=True), state[3])
        e = jnp.exp2(p - mp)
        old = jnp.exp2(state[0] - mp)
        sp = jnp.sum(e, axis=0, keepdims=True) + old * state[1]
        u = jnp.sum(e * d, axis=0, keepdims=True) + old * state[2]
        sq = jnp.sum(jnp.exp2(q - mq), axis=0, keepdims=True) + jnp.exp2(state[3] - mq) * state[4]
        return (mp, sp, u, mq, sq)

    low = jnp.full((1, columns), -1e30, F32)
    zero = jnp.zeros((1, columns), F32)
    blocks = 2 * own_ref.shape[0] // BLOCK
    mp, sp, u, mq, sq = lax.fori_loop(0, blocks, step, (low, zero, zero, low, zero))
    return stack_rows(mp + jnp.log2(sp), mq + jnp.log2(sq), u / sp, (8, columns))


def tile_stats(own, other, halves, old):
    pairs = len(halves) // 2
    half = halves[0].shape
    columns = len(halves) * half[0]
    rows = 2 * own.shape[0]
    args = [own, other, *halves] + ([] if old is None else [old])
    tile = jax.ShapeDtypeStruct((rows, half[0]), F32)
    row, col, *tiles = call(
        lambda *refs: stats_kernel(pairs, old is not None, *refs),
        (jax.ShapeDtypeStruct((8, rows), F32), jax.ShapeDtypeStruct((8, columns), F32), *[tile] * (2 * len(halves))),
        args,
        2 * rows * columns * own.shape[1],
        scratch=[
            pltpu.VMEM((BLOCK, half[1]), BF16),
            pltpu.VMEM(half, BF16),
            pltpu.VMEM(half, BF16),
            pltpu.VMEM((8, rows), F32),
        ],
    )
    return row, col, [tiles[n : n + 2] for n in range(0, len(tiles), 2)]


def merge(parts):
    top = parts[0]
    for part in parts[1:]:
        top = jnp.maximum(top, part)
    weights = [jnp.exp2(part - top) for part in parts]
    total = sum(weights)
    mean = sum(pltpu.roll(w, 2, 0) * part for w, part in zip(weights, parts)) / pltpu.roll(total, 2, 0)
    sub = lax.broadcasted_iota(jnp.int32, top.shape, 0)
    return jnp.where((sub == 2) | (sub == 5), mean, top + jnp.log2(total))


def on_core(core):
    return pl.when(lax.rem(lax.axis_index("col"), CORES) == core)


def lanes(*index):
    at = 0
    for i in index:
        at = at * SIDE + i
    return slice(at * 128, (at + 1) * 128)


def rows_3(first, second):
    return jnp.concatenate([first[:3], second[:3], first[:2]], axis=0)


def local_kernel(row_ref, near_ref, far_ref, out_ref):
    def columns(second, first):
        if second == 2:
            return far_ref[:, lanes(first)]
        half, at = divmod(first, SIDE // 2)
        return near_ref[:, lanes({0: (0, 2), 1: (4, 8), 3: (6, 10)}[second][half] + at)]

    for core in range(CORES):

        @on_core(core)
        def _():
            for x in range(SIDE):
                for y in range(SIDE):
                    col = columns(y, x) if core == 0 else columns(x, y)
                    row = col
                    if x < CORES:
                        row = row_ref[:, lanes(x if core == 0 else 1 - x, y)]
                    out_ref[:, lanes(x, y)] = rows_3(col, row)


def chip_kernel(own_ref, got_ref, out_ref):
    @on_core(0)
    def _():
        out_ref[...] = rows_3(own_ref[...], got_ref[...])

    @on_core(1)
    def _():
        rows = merge([jnp.concatenate([r[3:6, :1024], r[3:6, :1024], r[:2, :1024]], axis=0) for r in (own_ref, got_ref)])
        out_ref[...] = jnp.zeros(out_ref.shape, F32)
        for z in range(SIDE):
            out_ref[:, lanes(z, 0)] = rows_3(rows[:, lanes(0, z)], rows[:, lanes(1, z)])


def line_kernel(own_ref, g1, g2, g3, out_ref):
    width = own_ref.shape[1] // SIDE
    got = (own_ref, g1, g2, g3)
    for n in range(SIDE):
        parts = [got[e][:, (n ^ e) * width : ((n ^ e) + 1) * width] for e in range(SIDE)]
        out_ref[:, n * width : (n + 1) * width] = merge(parts)


def split_kernel(own_ref, got_ref, col_ref, row_ref):
    for core in range(CORES):

        @on_core(core)
        def _():
            cols, rows = (own_ref, got_ref) if core == 0 else (got_ref, own_ref)
            col_ref[...] = rows_3(cols[3 * core :, :][:3], cols[3 * core :, :][:3])
            for k in range(CORES):
                first = 3 * (k ^ core)
                for z in range(SIDE):
                    part = rows[:, lanes(z, 0)][first : first + 3]
                    row_ref[:, lanes(k, z)] = rows_3(part, part)


def plane_kernel(own_ref, g1, g2, g3, row_ref, out_ref, row_tail_ref, col_tail_ref, lowest_ref):
    got = (own_ref, g1, g2, g3)
    for x in range(SIDE):
        for y in range(SIDE):
            part = merge([got[e][:, lanes(x, y ^ e)] for e in range(SIDE)])

            @on_core(0)
            def _():
                out_ref[:, lanes(y, x)] = part

            @on_core(1)
            def _():
                out_ref[:, lanes(x, y)] = part

    put_tail(row_tail_ref, 0, kl_sum(row_ref[...]))
    put_tail(col_tail_ref, 0, kl_sum(out_ref[...]))
    lowest = jnp.minimum(
        jnp.min(row_ref[0:2, :], axis=1, keepdims=True), jnp.min(out_ref[0:2, :], axis=1, keepdims=True)
    )
    lowest_ref[...] = jnp.broadcast_to(jnp.min(lowest, axis=0, keepdims=True), lowest_ref.shape)


def exchange(row, cols):
    columns = sum(col.shape[1] for col in cols)
    out = jax.ShapeDtypeStruct((8, columns), F32)
    tail = jax.ShapeDtypeStruct((TAIL, columns // SIDE), BF16)
    local = call(local_kernel, out, (row, *cols))
    chip = call(chip_kernel, out, (local, send(local, other_core())))
    line = call(line_kernel, out, (chip, *(send(chip, x_or_z(e)) for e in ORDER)))
    col, row = call(split_kernel, (out, jax.ShapeDtypeStruct(row.shape, F32)), (line, send(line, other_core())))
    parts = [send(col, along_y(e)) for e in ORDER]
    col, *rest = call(plane_kernel, (out, tail, tail, jax.ShapeDtypeStruct((8, 128), F32)), (col, *parts, row))
    return row, col, *rest


def kl_sum(stats):
    kl = stats[2:3, :] - (stats[0:1, :] - stats[1:2, :])
    return jnp.sum(kl, axis=1, keepdims=True)


def put_tail(ref, at, value):
    shape = (TAIL, ref.shape[1])
    rest = jnp.broadcast_to(value, shape)
    sub = lax.broadcasted_iota(jnp.int32, shape, 0)
    tail = jnp.zeros(shape, F32)
    for n in range(3):
        part = rest.astype(BF16).astype(F32)
        tail = jnp.where(sub == n, part, tail)
        rest = rest - part
    ref[at : at + TAIL, :] = tail.astype(BF16)


def get_tail(ref, at):
    return jnp.sum(ref[at : at + TAIL, :].astype(F32), axis=0, keepdims=True)


def grad_kernel(piece, own_ref, other_ref, low_ref, high_ref, row_ref, col_ref, lowest_ref, *refs):
    ep_low, eq_low, ep_high, eq_high, *tail, g_ref, out_ref, block_ref = refs
    txt_refs = (low_ref, high_ref)
    columns = g_ref.shape[1]
    width = own_ref.shape[1] // 2
    half = own_ref.shape[0]
    blocks = 2 * half // BLOCK
    stats = col_ref[:, piece * columns : (piece + 1) * columns]
    lowest = lowest_ref[0, 0]

    def turned(n, x):
        out = []
        for k in range(BLOCK // 128):
            at = pl.multiple_of(n * BLOCK + k * 128, 128)
            out.append(jnp.concatenate([x(row_ref[:, pl.ds(at, 128)])] * 16, axis=0).T)
        out = jnp.concatenate(out, axis=0)
        return out[:, 0:1], out[:, 1:2]

    @pl.when(lowest >= LOWEST)
    def _():
        col = jnp.exp2(SHIFT - 1.0 - stats)

        def step(n, _):
            span = pl.ds(pl.multiple_of(n * BLOCK, BLOCK), BLOCK)
            rp, rq = turned(n, lambda x: jnp.exp2(SHIFT - 1.0 - x))
            ep = jnp.concatenate([ep_low[span, :], ep_high[span, :]], axis=1)
            eq = jnp.concatenate([eq_low[span, :], eq_high[span, :]], axis=1)
            g = eq * (rq + col[1:2, :]) - ep * (rp + col[0:1, :])
            g_ref[span, :] = g.astype(BF16)
            return 0

        lax.fori_loop(0, blocks, step, 0, unroll=True)

    @pl.when(lowest < LOWEST)
    def _():
        cp = stats[0:1, :] + 1.0
        cq = stats[1:2, :] + 1.0

        def step(n, _):
            load_block(n, own_ref, other_ref, block_ref)
            rp, rq = turned(n, lambda x: x + 1.0)
            p, q = logits(block_ref[...], txt_refs)
            g = (jnp.exp2(q - rq) - jnp.exp2(p - rp)) + (jnp.exp2(q - cq) - jnp.exp2(p - cp))
            g_ref[pl.ds(pl.multiple_of(n * BLOCK, BLOCK), BLOCK), :] = g.astype(BF16)
            return 0

        lax.fori_loop(0, blocks, step, 0)

    total = dot(g_ref[:half, :], own_ref[:, :width], TN) + dot(g_ref[half:, :], other_ref[:, :width], TN)
    out_ref[:columns, :] = total.astype(out_ref.dtype)
    if tail:
        out_ref[columns:, :] = tail[0][...]


def tile_grad(own, other, txt, tiles, stats, piece):
    row, col, row_tail, _, lowest = stats
    rows = own.shape[0] + other.shape[0]
    columns, width = 2 * txt[0].shape[0], own.shape[1]
    shape = jax.ShapeDtypeStruct
    out = shape((columns + TAIL, width // 2), BF16) if piece else shape((columns, width // 2), F32)
    return call(
        lambda *refs: grad_kernel(piece, *refs),
        (shape((rows, columns), BF16), out),
        (own, other, *txt, row, col, lowest, *tiles) + ((row_tail,) if piece else ()),
        0,
        scratch=[pltpu.VMEM((BLOCK, width), BF16)],
    )


def image_rows(first, half, grad_refs, txt_refs, store):
    rows, width = txt_refs[0].shape
    width //= 2

    def step(n, _):
        at = pl.multiple_of(n * BLOCK, BLOCK)
        total = None
        for m, txt_ref in enumerate(txt_refs):
            at_column = m % 2 * rows
            part = dot(grad_refs[m // 2][pl.ds(first + at, BLOCK), at_column : at_column + rows], txt_ref[:, :width])
            total = part if total is None else total + part
        store(pl.ds(at, BLOCK), total)
        return 0

    lax.fori_loop(0, half // BLOCK, step, 0, unroll=True)


def other_images_kernel(*refs):
    tail_ref, out_ref = refs[3 * SIDE :]
    half = out_ref.shape[0] - TAIL

    def store(span, value):
        out_ref[span, :] = value.astype(BF16)

    image_rows(half, half, refs[:SIDE], refs[SIDE : 3 * SIDE], store)
    out_ref[half:, :] = tail_ref[...]


def own_images_kernel(*refs):
    out_ref = refs[-1]

    def store(span, value):
        out_ref[span, :] = value

    image_rows(0, out_ref.shape[0], refs[:SIDE], refs[SIDE : 3 * SIDE], store)


def image_grads(grads, txts, tail):
    rows, columns = grads[0].shape
    txts = [half for piece in txts for half in piece]
    width = txts[0].shape[1] // 2
    half = rows // 2
    shape = jax.ShapeDtypeStruct
    flops = 0
    message = call(other_images_kernel, shape((half + TAIL, width), BF16), (*grads, *txts, tail), flops)
    return message, call(own_images_kernel, shape((half, width), F32), (*grads, *txts), flops)


def combine_kernel(count, own_ref, tail_ref, *refs):
    got, outs = refs[:count], refs[-SIDE:]
    size = own_ref.shape[0]
    step = size // SIDE
    value = get_tail(tail_ref, 0) + sum(get_tail(ref, size) for ref in got)
    for n, ref in enumerate(outs):
        span = slice(n * step, (n + 1) * step)
        total = own_ref[span, :]
        for part in got:
            total = total + part[span, :].astype(F32)
        ref[:step, :] = total.astype(ref.dtype)
        if n:
            put_tail(ref, step, value)
        else:
            ref[step:, :] = jnp.broadcast_to(value, (8, value.shape[1]))


def combine(own, tail, got, after=()):
    size, width = own.shape
    step = size // SIDE
    message = jax.ShapeDtypeStruct((step + TAIL, width), BF16)
    keep = jax.ShapeDtypeStruct((step + 8, width), F32)
    return call(
        lambda *refs: combine_kernel(len(got), *refs),
        (keep, message, message, message),
        (own, tail, *got, *after),
        hbm=-len(after),
    )


def tangent(x_ref, keep_ref, got, grad_ref):
    rows = x_ref.shape[0]
    u, n = unit_rows(x_ref[...])
    du = scale * (keep_ref[:rows, :] + sum(ref[:rows, :].astype(F32) for ref in got))
    grad_ref[...] = (du - u * jnp.sum(u * du, axis=-1, keepdims=True)) / n
    return keep_ref[rows : rows + 1, :] + sum(get_tail(ref, rows) for ref in got)


def finish_kernel(factor, *refs):
    *ins, grad_image_ref, grad_text_ref, loss_ref = refs
    each = len(ins) // 2
    value = jnp.zeros((1, grad_text_ref.shape[1]), F32)
    for n, grad_ref in enumerate((grad_image_ref, grad_text_ref)):
        x_ref, keep_ref, *got = ins[n * each : (n + 1) * each]
        value = value + tangent(x_ref, keep_ref, got, grad_ref)
    loss_ref[0, 0] = factor * jnp.max(value)


def finish(image, text, factor):
    loss = jax.ShapeDtypeStruct((1, 1), F32)
    out = tuple(jax.ShapeDtypeStruct(x.shape, F32) for x in (image[0], text[0])) + (loss,)
    return call(lambda *refs: finish_kernel(factor, *refs), out, (*image, *text))


def shards(image_student, text_student, image_teacher, text_teacher, sketch):
    rows, width = image_student.shape
    txt = prepare(text_student, text_teacher, sketch, True)

    blocks = [txt] + [send(txt, first(e)) for e in range(1, SIDE)]
    img = prepare(image_student, image_teacher, sketch, False, (blocks[1],))
    img_1, img_3 = send(img, along_z(1)), send(img, along_z(3))
    low, high = lay_end([blocks[:2], blocks[2:]], (img_1, img_3))
    low_1, low_3 = send(low, second(1)), send(low, second(3))
    high_1, high_3 = send(high, second(1)), send(high, second(3))
    low_2, high_2 = send(low_3, second(1)), send(high_1, second(3))
    txt_all = [(low, high), (low_1, high_1), (low_2, high_2), (low_3, high_3)]
    (own,) = lay_end([[img, img_1, send(img, along_z(2)), img_3]], (low_1, low_3, high_1, high_3))
    other = send(own, other_core())

    row, near_col, near = tile_stats(own, other, (low, high, low_1, low_3, high_1, high_3), None)
    row, far_col, far = tile_stats(own, other, (low_2, high_2), row)
    tiles = [near[0] + near[1], near[2] + near[4], far[0] + far[1], near[3] + near[5]]
    stats = exchange(row, (near_col, far_col))

    grads, got = [None] * SIDE, []
    for b in (2, 1, 3):
        grads[b], message = tile_grad(own, other, txt_all[b], tiles[b], stats, b)
        got.append(send(message, second(b)))
    grads[0], own_txt = tile_grad(own, other, txt_all[0], tiles[0], stats, 0)
    message, own_img = image_grads(grads, txt_all, stats[3])
    keep, *messages = combine(own_img, stats[3], [send(message, other_core())])
    image = [image_student, keep] + [send(messages[e - 1], along_z(e)) for e in (3, 2, 1)]
    keep_txt, *messages_txt = combine(own_txt, stats[2], got, image[2:3])
    text = [text_student, keep_txt] + [send(messages_txt[e - 1], first(e)) for e in (3, 2, 1)]
    pairs = rows * lax.axis_size("row") * lax.axis_size("col")
    grad_image, grad_text, mean_loss = finish(image, text, 0.5 / (LOG2E * pairs))
    return (grad_image, grad_text, mean_loss.reshape(()))


def solution(mesh):
    return jax.shard_map(
        shards,
        mesh=mesh,
        in_specs=(
            P(("row", "col"), None),
            P(("col", "row"), None),
            P(("row", "col"), None),
            P(("col", "row"), None),
            P(),
        ),
        out_specs=(P(("row", "col"), None), P(("col", "row"), None), P()),
        check_vma=False,
    )
```

```python
import math

import jax
import jax.numpy as jnp
from jax import lax
from jax.experimental import pallas as pl
from jax.experimental.pallas import tpu as pltpu
from jax.sharding import PartitionSpec as P

scale = 100.0
LOG2E = math.log2(math.e)
units = scale * LOG2E
SIDE = 4
CORES = 2
AXES = ("row", "col")
ORDER = (1, 2, 3)


def route(step):
    pairs = []
    for x in range(SIDE):
        for y in range(SIDE):
            for z in range(SIDE):
                for k in range(CORES):
                    a, b, c, d = step(x, y, z, k)
                    src = ((x * SIDE + y) * SIDE + z) * CORES + k
                    dst = ((a * SIDE + b) * SIDE + c) * CORES + d
                    pairs.append((src, dst))
    return pairs


def first(e):
    return route(lambda x, y, z, k: (x ^ e, y, z, k) if k == 0 else (x, y ^ e, z, k))


def second(e):
    return route(lambda x, y, z, k: (x, y ^ e, z, k) if k == 0 else (x ^ e, y, z, k))


def along_z(e):
    return route(lambda x, y, z, k: (x, y, z ^ e, k))


def x_or_z(e):
    return route(lambda x, y, z, k: (x ^ e, y, z, k) if k == 0 else (x, y, z ^ e, k))


def along_y(e):
    return route(lambda x, y, z, k: (x, y ^ e, z, k))


def other_core():
    return route(lambda x, y, z, k: (x, y, z, k ^ 1))


def send(x, pairs):
    return lax.ppermute(x, AXES, pairs)


BF16 = jnp.bfloat16
F32 = jnp.float32
NT = (((1,), (1,)), ((), ()))
TN = (((0,), (0,)), ((), ()))
VMEM_LIMIT = 16 * 1024 * 1024
FIRST_LIMIT = 56 * 1024 * 1024
TAIL = 16
BLOCK = 256
SHIFT = 34.0
LOWEST = -60.0


def dot(a, b, dims=(((1,), (0,)), ((), ()))):
    return lax.dot_general(a, b, dims, preferred_element_type=F32)


def call(kernel, out_shape, args, flops=0, scratch=(), hbm=0, limit=VMEM_LIMIT):
    size = sum(a.size * a.dtype.itemsize for a in args)
    size += sum(math.prod(o.shape) * o.dtype.itemsize for o in jax.tree.leaves(out_shape))
    size = size if flops else 0
    return pl.pallas_call(
        kernel,
        out_shape=out_shape,
        in_specs=(
            [pl.BlockSpec(memory_space=pltpu.HBM)] * max(hbm, 0)
            + [pl.BlockSpec(memory_space=pltpu.VMEM)] * (len(args) - abs(hbm))
            + [pl.BlockSpec(memory_space=pl.ANY)] * max(-hbm, 0)
        ),
        out_specs=jax.tree.map(
            lambda o: pl.BlockSpec(memory_space=pltpu.SMEM if o.shape == (1, 1) else pltpu.VMEM), out_shape
        ),
        scratch_shapes=scratch,
        compiler_params=pltpu.CompilerParams(vmem_limit_bytes=limit),
        cost_estimate=pl.CostEstimate(flops=flops, bytes_accessed=size, transcendentals=0),
    )(*args)


def unit_rows(x):
    x32 = x.astype(F32)
    norms = jnp.sqrt(jnp.sum(x32 * x32, axis=-1, keepdims=True) + 1e-06)
    return (x32 / norms, norms)


def unit_block(student, teacher, sketch, out_ref):
    width = student.shape[1]
    out_ref[:, :width] = unit_rows(student)[0].astype(BF16)
    out_ref[:, width:] = unit_rows(dot(teacher, sketch))[0].astype(BF16)


def prepare_first_kernel(student_hbm, teacher_hbm, sketch_hbm, out_ref, *refs):
    *buffers, sems = refs
    copies = [
        pltpu.make_async_copy(src, dst, sems.at[n])
        for n, (src, dst) in enumerate(zip((student_hbm, teacher_hbm, sketch_hbm), buffers))
    ]
    for copy in copies:
        copy.start()
    for copy in copies:
        copy.wait()
    unit_block(*(ref[...] for ref in buffers), out_ref)


def prepare_kernel(student_ref, teacher_ref, sketch_ref, *refs):
    out_ref = refs[-1]
    unit_block(student_ref[...], teacher_ref[...], sketch_ref[...], out_ref)


def prepare(student, teacher, sketch, first_kernel, after=()):
    rows, width = student.shape
    out = jax.ShapeDtypeStruct((rows, 2 * width), BF16)
    args = (student, teacher, sketch)
    flops = 2 * rows * sketch.size
    if not first_kernel:
        return call(prepare_kernel, out, (*args, *after), flops, hbm=-len(after))
    scratch = [pltpu.VMEM(x.shape, x.dtype) for x in args] + [pltpu.SemaphoreType.DMA((len(args),))]
    return call(prepare_first_kernel, out, args, flops, scratch, hbm=3, limit=FIRST_LIMIT)


def lay_end_kernel(count, sizes, *refs):
    blocks = iter(refs[:count])
    for size, out_ref in zip(sizes, refs[count:]):
        at = 0
        for ref in (next(blocks) for _ in range(size)):
            out_ref[at : at + ref.shape[0], :] = ref[...]
            at += ref.shape[0]


def lay_end(groups, after=()):
    width = groups[0][0].shape[1]
    out = [jax.ShapeDtypeStruct((sum(block.shape[0] for block in group), width), BF16) for group in groups]
    args = [block for group in groups for block in group] + list(after)
    sizes = [len(group) for group in groups]
    return call(lambda *refs: lay_end_kernel(len(args), sizes, *refs), out, args, hbm=-len(after))


def products(img, txt_refs):
    width = img.shape[1] // 2
    p = [dot(img[:, width:], ref[:, width:], NT) for ref in txt_refs]
    q = [dot(img[:, :width], ref[:, :width], NT) for ref in txt_refs]
    return jnp.concatenate(p, axis=1), jnp.concatenate(q, axis=1)


def logits(img, txt_refs):
    p, q = products(img, txt_refs)
    return units * p, units * q


def load_block(n, own_ref, other_ref, block_ref):
    half = own_ref.shape[0] // BLOCK

    @pl.when(n < half)
    def _():
        block_ref[...] = own_ref[pl.ds(pl.multiple_of(n * BLOCK, BLOCK), BLOCK), :]

    @pl.when(n >= half)
    def _():
        block_ref[...] = other_ref[pl.ds(pl.multiple_of((n - half) * BLOCK, BLOCK), BLOCK), :]


def put_rows(row_ref, n, first, second, third):
    lane = lax.broadcasted_iota(jnp.int32, (BLOCK, 128), 1)
    packed = jnp.where(lane == 0, first, jnp.where(lane == 1, second, third))
    for k in range(BLOCK // 128):
        at = pl.multiple_of(n * BLOCK + k * 128, 128)
        row_ref[:, pl.ds(at, 128)] = packed[k * 128 : (k + 1) * 128].T[:8]


def put_sums(row_ref, n, *tiles):
    for k in range(BLOCK // 128):
        sums = [jnp.sum(tile[k * 128 : (k + 1) * 128].T, axis=0, keepdims=True) for tile in tiles]
        at = pl.multiple_of(n * BLOCK + k * 128, 128)
        row_ref[:, pl.ds(at, 128)] = stack_rows(*sums, (8, 128))


def stack_rows(first, second, third, shape):
    sub = lax.broadcasted_iota(jnp.int32, shape, 0)
    return jnp.where(sub == 0, first, jnp.where(sub == 1, second, third))


def merge_rows(new, old):
    top = jnp.maximum(new, old)
    new_w, old_w = jnp.exp2(new - top), jnp.exp2(old - top)
    total = new_w + old_w
    mean = (new_w[0:1] * new + old_w[0:1] * old) / total[0:1]
    lse = top + jnp.log2(total)
    return stack_rows(lse, lse, mean, new.shape)


def stats_kernel(pairs, has_old, own_ref, other_ref, *refs):
    halves, refs = refs[: 2 * pairs], refs[2 * pairs :]
    old_ref = refs[0] if has_old else None
    row_ref, col_ref, *tile_refs, block_ref, low_ref, high_ref, part_ref = refs[int(has_old) :]
    columns = col_ref.shape[1] // pairs
    blocks = 2 * own_ref.shape[0] // BLOCK

    def step(n, state):
        load_block(n, own_ref, other_ref, block_ref)
        row_sums, out = None, []
        for m in range(pairs):
            p, q = products(block_ref[...], halves[2 * m : 2 * m + 2])
            ep = jnp.exp2(units * p - SHIFT)
            eq = jnp.exp2(units * q - SHIFT)
            tiles = (ep, eq, ep * (p - q))
            span = pl.ds(pl.multiple_of(n * BLOCK, BLOCK), BLOCK)
            for k in range(4):
                at = k // 2 * (columns // 2)
                tile_refs[4 * m + k][span, :] = tiles[k % 2][:, at : at + columns // 2]
            out += [s + jnp.sum(x, axis=0, keepdims=True) for s, x in zip(state[3 * m : 3 * m + 3], tiles)]
            part = [sum(x[:, c : c + 128] for c in range(0, columns, 128)) for x in tiles]
            row_sums = part if row_sums is None else [x + y for x, y in zip(row_sums, part)]
        put_sums(row_ref, n, *row_sums)
        return tuple(out)

    zero = jnp.zeros((1, columns), F32)
    state = lax.fori_loop(0, blocks, step, (zero,) * (3 * pairs), unroll=pairs == 1)
    rows = row_ref[...]
    lowest = jnp.min(rows[0:2, :])
    for m in range(pairs):
        sp, sq, u = state[3 * m : 3 * m + 3]
        lowest = jnp.minimum(lowest, jnp.min(jnp.minimum(sp, sq)))
        col_ref[:, m * columns : (m + 1) * columns] = stack_rows(
            SHIFT + jnp.log2(sp), SHIFT + jnp.log2(sq), units * u / sp, (8, columns)
        )
    row_ref[...] = stack_rows(SHIFT + jnp.log2(rows), SHIFT + jnp.log2(rows), units * rows / rows[0:1], rows.shape)

    @pl.when(lowest < 2.0 ** (LOWEST - SHIFT))
    def _():
        def pair(m, _):
            for n in range(pairs):

                @pl.when(m == n)
                def _():
                    low_ref[...] = halves[2 * n][...]
                    high_ref[...] = halves[2 * n + 1][...]

            col = careful_stats(own_ref, other_ref, (low_ref, high_ref), part_ref, columns, block_ref)
            col_ref[:, pl.ds(pl.multiple_of(m * columns, columns), columns)] = col

            @pl.when(m == 0)
            def _():
                row_ref[...] = part_ref[...]

            @pl.when(m > 0)
            def _():
                row_ref[...] = merge_rows(part_ref[...], row_ref[...])

            return 0

        lax.fori_loop(0, pairs, pair, 0)

    if has_old:
        row_ref[...] = merge_rows(row_ref[...], old_ref[...])


def careful_stats(own_ref, other_ref, txt_refs, row_ref, columns, block_ref):

    def step(n, state):
        load_block(n, own_ref, other_ref, block_ref)
        p, q = logits(block_ref[...], txt_refs)
        d = p - q
        mp = jnp.max(p, axis=1, keepdims=True)
        mq = jnp.max(q, axis=1, keepdims=True)
        e = jnp.exp2(p - mp)
        sp = jnp.sum(e, axis=1, keepdims=True)
        u = jnp.sum(e * d, axis=1, keepdims=True)
        sq = jnp.sum(jnp.exp2(q - mq), axis=1, keepdims=True)
        put_rows(row_ref, n, mp + jnp.log2(sp), mq + jnp.log2(sq), u / sp)
        mp = jnp.maximum(jnp.max(p, axis=0, keepdims=True), state[0])
        mq = jnp.maximum(jnp.max(q, axis=0, keepdims=True), state[3])
        e = jnp.exp2(p - mp)
        old = jnp.exp2(state[0] - mp)
        sp = jnp.sum(e, axis=0, keepdims=True) + old * state[1]
        u = jnp.sum(e * d, axis=0, keepdims=True) + old * state[2]
        sq = jnp.sum(jnp.exp2(q - mq), axis=0, keepdims=True) + jnp.exp2(state[3] - mq) * state[4]
        return (mp, sp, u, mq, sq)

    low = jnp.full((1, columns), -1e30, F32)
    zero = jnp.zeros((1, columns), F32)
    blocks = 2 * own_ref.shape[0] // BLOCK
    mp, sp, u, mq, sq = lax.fori_loop(0, blocks, step, (low, zero, zero, low, zero))
    return stack_rows(mp + jnp.log2(sp), mq + jnp.log2(sq), u / sp, (8, columns))


def tile_stats(own, other, halves, old):
    pairs = len(halves) // 2
    half = halves[0].shape
    columns = len(halves) * half[0]
    rows = 2 * own.shape[0]
    args = [own, other, *halves] + ([] if old is None else [old])
    tile = jax.ShapeDtypeStruct((rows, half[0]), F32)
    row, col, *tiles = call(
        lambda *refs: stats_kernel(pairs, old is not None, *refs),
        (jax.ShapeDtypeStruct((8, rows), F32), jax.ShapeDtypeStruct((8, columns), F32), *[tile] * (2 * len(halves))),
        args,
        2 * rows * columns * own.shape[1],
        scratch=[
            pltpu.VMEM((BLOCK, half[1]), BF16),
            pltpu.VMEM(half, BF16),
            pltpu.VMEM(half, BF16),
            pltpu.VMEM((8, rows), F32),
        ],
    )
    return row, col, [tiles[n : n + 2] for n in range(0, len(tiles), 2)]


def merge(parts):
    top = parts[0]
    for part in parts[1:]:
        top = jnp.maximum(top, part)
    weights = [jnp.exp2(part - top) for part in parts]
    total = sum(weights)
    mean = sum(pltpu.roll(w, 2, 0) * part for w, part in zip(weights, parts)) / pltpu.roll(total, 2, 0)
    sub = lax.broadcasted_iota(jnp.int32, top.shape, 0)
    return jnp.where((sub == 2) | (sub == 5), mean, top + jnp.log2(total))


def on_core(core):
    return pl.when(lax.rem(lax.axis_index("col"), CORES) == core)


def lanes(*index):
    at = 0
    for i in index:
        at = at * SIDE + i
    return slice(at * 128, (at + 1) * 128)


def rows_3(first, second):
    return jnp.concatenate([first[:3], second[:3], first[:2]], axis=0)


def local_kernel(row_ref, near_ref, far_ref, out_ref):
    def columns(second, first):
        if second == 2:
            return far_ref[:, lanes(first)]
        half, at = divmod(first, SIDE // 2)
        return near_ref[:, lanes({0: (0, 2), 1: (4, 8), 3: (6, 10)}[second][half] + at)]

    for core in range(CORES):

        @on_core(core)
        def _():
            for x in range(SIDE):
                for y in range(SIDE):
                    col = columns(y, x) if core == 0 else columns(x, y)
                    row = col
                    if x < CORES:
                        row = row_ref[:, lanes(x if core == 0 else 1 - x, y)]
                    out_ref[:, lanes(x, y)] = rows_3(col, row)


def chip_kernel(own_ref, got_ref, out_ref):
    @on_core(0)
    def _():
        out_ref[...] = rows_3(own_ref[...], got_ref[...])

    @on_core(1)
    def _():
        rows = merge([jnp.concatenate([r[3:6, :1024], r[3:6, :1024], r[:2, :1024]], axis=0) for r in (own_ref, got_ref)])
        out_ref[...] = jnp.zeros(out_ref.shape, F32)
        for z in range(SIDE):
            out_ref[:, lanes(z, 0)] = rows_3(rows[:, lanes(0, z)], rows[:, lanes(1, z)])


def line_kernel(own_ref, g1, g2, g3, out_ref):
    width = own_ref.shape[1] // SIDE
    got = (own_ref, g1, g2, g3)
    for n in range(SIDE):
        parts = [got[e][:, (n ^ e) * width : ((n ^ e) + 1) * width] for e in range(SIDE)]
        out_ref[:, n * width : (n + 1) * width] = merge(parts)


def split_kernel(own_ref, got_ref, col_ref, row_ref):
    for core in range(CORES):

        @on_core(core)
        def _():
            cols, rows = (own_ref, got_ref) if core == 0 else (got_ref, own_ref)
            col_ref[...] = rows_3(cols[3 * core :, :][:3], cols[3 * core :, :][:3])
            for k in range(CORES):
                first = 3 * (k ^ core)
                for z in range(SIDE):
                    part = rows[:, lanes(z, 0)][first : first + 3]
                    row_ref[:, lanes(k, z)] = rows_3(part, part)


def plane_kernel(own_ref, g1, g2, g3, row_ref, out_ref, row_tail_ref, col_tail_ref, lowest_ref):
    got = (own_ref, g1, g2, g3)
    for x in range(SIDE):
        for y in range(SIDE):
            part = merge([got[e][:, lanes(x, y ^ e)] for e in range(SIDE)])

            @on_core(0)
            def _():
                out_ref[:, lanes(y, x)] = part

            @on_core(1)
            def _():
                out_ref[:, lanes(x, y)] = part

    put_tail(row_tail_ref, 0, kl_sum(row_ref[...]))
    put_tail(col_tail_ref, 0, kl_sum(out_ref[...]))
    lowest = jnp.minimum(
        jnp.min(row_ref[0:2, :], axis=1, keepdims=True), jnp.min(out_ref[0:2, :], axis=1, keepdims=True)
    )
    lowest_ref[...] = jnp.broadcast_to(jnp.min(lowest, axis=0, keepdims=True), lowest_ref.shape)


def exchange(row, cols):
    columns = sum(col.shape[1] for col in cols)
    out = jax.ShapeDtypeStruct((8, columns), F32)
    tail = jax.ShapeDtypeStruct((TAIL, columns // SIDE), BF16)
    local = call(local_kernel, out, (row, *cols))
    chip = call(chip_kernel, out, (local, send(local, other_core())))
    line = call(line_kernel, out, (chip, *(send(chip, x_or_z(e)) for e in ORDER)))
    col, row = call(split_kernel, (out, jax.ShapeDtypeStruct(row.shape, F32)), (line, send(line, other_core())))
    parts = [send(col, along_y(e)) for e in ORDER]
    col, *rest = call(plane_kernel, (out, tail, tail, jax.ShapeDtypeStruct((8, 128), F32)), (col, *parts, row))
    return row, col, *rest


def kl_sum(stats):
    kl = stats[2:3, :] - (stats[0:1, :] - stats[1:2, :])
    return jnp.sum(kl, axis=1, keepdims=True)


def put_tail(ref, at, value):
    shape = (TAIL, ref.shape[1])
    rest = jnp.broadcast_to(value, shape)
    sub = lax.broadcasted_iota(jnp.int32, shape, 0)
    tail = jnp.zeros(shape, F32)
    for n in range(3):
        part = rest.astype(BF16).astype(F32)
        tail = jnp.where(sub == n, part, tail)
        rest = rest - part
    ref[at : at + TAIL, :] = tail.astype(BF16)


def get_tail(ref, at):
    return jnp.sum(ref[at : at + TAIL, :].astype(F32), axis=0, keepdims=True)


def grad_kernel(piece, own_ref, other_ref, low_ref, high_ref, row_ref, col_ref, lowest_ref, *refs):
    ep_low, eq_low, ep_high, eq_high, *tail, g_ref, out_ref, block_ref = refs
    txt_refs = (low_ref, high_ref)
    columns = g_ref.shape[1]
    width = own_ref.shape[1] // 2
    half = own_ref.shape[0]
    blocks = 2 * half // BLOCK
    stats = col_ref[:, piece * columns : (piece + 1) * columns]
    lowest = lowest_ref[0, 0]

    def turned(n, x):
        out = []
        for k in range(BLOCK // 128):
            at = pl.multiple_of(n * BLOCK + k * 128, 128)
            out.append(jnp.concatenate([x(row_ref[:, pl.ds(at, 128)])] * 16, axis=0).T)
        out = jnp.concatenate(out, axis=0)
        return out[:, 0:1], out[:, 1:2]

    @pl.when(lowest >= LOWEST)
    def _():
        col = jnp.exp2(SHIFT - 1.0 - stats)

        def step(n, _):
            span = pl.ds(pl.multiple_of(n * BLOCK, BLOCK), BLOCK)
            rp, rq = turned(n, lambda x: jnp.exp2(SHIFT - 1.0 - x))
            ep = jnp.concatenate([ep_low[span, :], ep_high[span, :]], axis=1)
            eq = jnp.concatenate([eq_low[span, :], eq_high[span, :]], axis=1)
            g = eq * (rq + col[1:2, :]) - ep * (rp + col[0:1, :])
            g_ref[span, :] = g.astype(BF16)
            return 0

        lax.fori_loop(0, blocks, step, 0, unroll=True)

    @pl.when(lowest < LOWEST)
    def _():
        cp = stats[0:1, :] + 1.0
        cq = stats[1:2, :] + 1.0

        def step(n, _):
            load_block(n, own_ref, other_ref, block_ref)
            rp, rq = turned(n, lambda x: x + 1.0)
            p, q = logits(block_ref[...], txt_refs)
            g = (jnp.exp2(q - rq) - jnp.exp2(p - rp)) + (jnp.exp2(q - cq) - jnp.exp2(p - cp))
            g_ref[pl.ds(pl.multiple_of(n * BLOCK, BLOCK), BLOCK), :] = g.astype(BF16)
            return 0

        lax.fori_loop(0, blocks, step, 0)

    total = dot(g_ref[:half, :], own_ref[:, :width], TN) + dot(g_ref[half:, :], other_ref[:, :width], TN)
    out_ref[:columns, :] = total.astype(out_ref.dtype)
    if tail:
        out_ref[columns:, :] = tail[0][...]


def tile_grad(own, other, txt, tiles, stats, piece):
    row, col, row_tail, _, lowest = stats
    rows = own.shape[0] + other.shape[0]
    columns, width = 2 * txt[0].shape[0], own.shape[1]
    shape = jax.ShapeDtypeStruct
    out = shape((columns + TAIL, width // 2), BF16) if piece else shape((columns, width // 2), F32)
    return call(
        lambda *refs: grad_kernel(piece, *refs),
        (shape((rows, columns), BF16), out),
        (own, other, *txt, row, col, lowest, *tiles) + ((row_tail,) if piece else ()),
        0,
        scratch=[pltpu.VMEM((BLOCK, width), BF16)],
    )


def image_rows(first, half, grad_refs, txt_refs, store):
    rows, width = txt_refs[0].shape
    width //= 2

    def step(n, _):
        at = pl.multiple_of(n * BLOCK, BLOCK)
        total = None
        for m, txt_ref in enumerate(txt_refs):
            at_column = m % 2 * rows
            part = dot(grad_refs[m // 2][pl.ds(first + at, BLOCK), at_column : at_column + rows], txt_ref[:, :width])
            total = part if total is None else total + part
        store(pl.ds(at, BLOCK), total)
        return 0

    lax.fori_loop(0, half // BLOCK, step, 0, unroll=True)


def other_images_kernel(*refs):
    tail_ref, out_ref = refs[3 * SIDE :]
    half = out_ref.shape[0] - TAIL

    def store(span, value):
        out_ref[span, :] = value.astype(BF16)

    image_rows(half, half, refs[:SIDE], refs[SIDE : 3 * SIDE], store)
    out_ref[half:, :] = tail_ref[...]


def own_images_kernel(*refs):
    out_ref = refs[-1]

    def store(span, value):
        out_ref[span, :] = value

    image_rows(0, out_ref.shape[0], refs[:SIDE], refs[SIDE : 3 * SIDE], store)


def image_grads(grads, txts, tail, after):
    rows, columns = grads[0].shape
    txts = [half for piece in txts for half in piece]
    width = txts[0].shape[1] // 2
    half = rows // 2
    shape = jax.ShapeDtypeStruct
    flops = 0
    message = call(other_images_kernel, shape((half + TAIL, width), BF16), (*grads, *txts, tail), flops)
    own = call(own_images_kernel, shape((half, width), F32), (*grads, *txts, *after), flops, hbm=-len(after))
    return message, own


def combine_kernel(count, own_ref, tail_ref, *refs):
    got, outs = refs[:count], refs[-SIDE:]
    size = own_ref.shape[0]
    step = size // SIDE
    value = get_tail(tail_ref, 0) + sum(get_tail(ref, size) for ref in got)
    for n, ref in enumerate(outs):
        span = slice(n * step, (n + 1) * step)
        total = own_ref[span, :]
        for part in got:
            total = total + part[span, :].astype(F32)
        ref[:step, :] = total.astype(ref.dtype)
        if n:
            put_tail(ref, step, value)
        else:
            ref[step:, :] = jnp.broadcast_to(value, (8, value.shape[1]))


def combine(own, tail, got, after=()):
    size, width = own.shape
    step = size // SIDE
    message = jax.ShapeDtypeStruct((step + TAIL, width), BF16)
    keep = jax.ShapeDtypeStruct((step + 8, width), F32)
    return call(
        lambda *refs: combine_kernel(len(got), *refs),
        (keep, message, message, message),
        (own, tail, *got, *after),
        hbm=-len(after),
    )


def tangent(x_ref, keep_ref, got, grad_ref):
    rows = x_ref.shape[0]
    u, n = unit_rows(x_ref[...])
    du = scale * (keep_ref[:rows, :] + sum(ref[:rows, :].astype(F32) for ref in got))
    grad_ref[...] = (du - u * jnp.sum(u * du, axis=-1, keepdims=True)) / n
    return keep_ref[rows : rows + 1, :] + sum(get_tail(ref, rows) for ref in got)


def finish_kernel(factor, *refs):
    *ins, grad_image_ref, grad_text_ref, loss_ref = refs
    each = len(ins) // 2
    value = jnp.zeros((1, grad_text_ref.shape[1]), F32)
    for n, grad_ref in enumerate((grad_image_ref, grad_text_ref)):
        x_ref, keep_ref, *got = ins[n * each : (n + 1) * each]
        value = value + tangent(x_ref, keep_ref, got, grad_ref)
    loss_ref[0, 0] = factor * jnp.max(value)


def finish(image, text, factor):
    loss = jax.ShapeDtypeStruct((1, 1), F32)
    out = tuple(jax.ShapeDtypeStruct(x.shape, F32) for x in (image[0], text[0])) + (loss,)
    return call(lambda *refs: finish_kernel(factor, *refs), out, (*image, *text))


def shards(image_student, text_student, image_teacher, text_teacher, sketch):
    rows, width = image_student.shape
    txt = prepare(text_student, text_teacher, sketch, True)

    blocks = [txt] + [send(txt, first(e)) for e in range(1, SIDE)]
    img = prepare(image_student, image_teacher, sketch, False, (blocks[1],))
    img_1, img_3 = send(img, along_z(1)), send(img, along_z(3))
    low, high = lay_end([blocks[:2], blocks[2:]], (img_1, img_3))
    low_1, low_3 = send(low, second(1)), send(low, second(3))
    high_1, high_3 = send(high, second(1)), send(high, second(3))
    low_2, high_2 = send(low_3, second(1)), send(high_1, second(3))
    txt_all = [(low, high), (low_1, high_1), (low_2, high_2), (low_3, high_3)]
    (own,) = lay_end([[img, img_1, send(img, along_z(2)), img_3]], (low_1, low_3, high_1, high_3))
    other = send(own, other_core())

    row, near_col, near = tile_stats(own, other, (low, high, low_1, low_3, high_1, high_3), None)
    row, far_col, far = tile_stats(own, other, (low_2, high_2), row)
    tiles = [near[0] + near[1], near[2] + near[4], far[0] + far[1], near[3] + near[5]]
    stats = exchange(row, (near_col, far_col))

    grads, got = [None] * SIDE, []
    for b in (3, 1, 2):
        grads[b], message = tile_grad(own, other, txt_all[b], tiles[b], stats, b)
        got.append(send(message, second(b)))
    grads[0], own_txt = tile_grad(own, other, txt_all[0], tiles[0], stats, 0)
    message, own_img = image_grads(grads, txt_all, stats[3], got[:2])
    keep, *messages = combine(own_img, stats[3], [send(message, other_core())])
    image = [image_student, keep] + [send(messages[e - 1], along_z(e)) for e in (3, 2, 1)]
    keep_txt, *messages_txt = combine(own_txt, stats[2], got, image[2:3])
    text = [text_student, keep_txt] + [send(messages_txt[e - 1], first(e)) for e in (3, 2, 1)]
    pairs = rows * lax.axis_size("row") * lax.axis_size("col")
    grad_image, grad_text, mean_loss = finish(image, text, 0.5 / (LOG2E * pairs))
    return (grad_image, grad_text, mean_loss.reshape(()))


def solution(mesh):
    return jax.shard_map(
        shards,
        mesh=mesh,
        in_specs=(
            P(("row", "col"), None),
            P(("col", "row"), None),
            P(("row", "col"), None),
            P(("col", "row"), None),
            P(),
        ),
        out_specs=(P(("row", "col"), None), P(("col", "row"), None), P()),
        check_vma=False,
    )
```

```python
import math

import jax
import jax.numpy as jnp
from jax import lax
from jax.experimental import pallas as pl
from jax.experimental.pallas import tpu as pltpu
from jax.sharding import PartitionSpec as P

scale = 100.0
LOG2E = math.log2(math.e)
units = scale * LOG2E
SIDE = 4
CORES = 2
AXES = ("row", "col")
ORDER = (1, 2, 3)


def route(step):
    pairs = []
    for x in range(SIDE):
        for y in range(SIDE):
            for z in range(SIDE):
                for k in range(CORES):
                    a, b, c, d = step(x, y, z, k)
                    src = ((x * SIDE + y) * SIDE + z) * CORES + k
                    dst = ((a * SIDE + b) * SIDE + c) * CORES + d
                    pairs.append((src, dst))
    return pairs


def first(e):
    return route(lambda x, y, z, k: (x ^ e, y, z, k) if k == 0 else (x, y ^ e, z, k))


def second(e):
    return route(lambda x, y, z, k: (x, y ^ e, z, k) if k == 0 else (x ^ e, y, z, k))


def along_z(e):
    return route(lambda x, y, z, k: (x, y, z ^ e, k))


def x_or_z(e):
    return route(lambda x, y, z, k: (x ^ e, y, z, k) if k == 0 else (x, y, z ^ e, k))


def along_y(e):
    return route(lambda x, y, z, k: (x, y ^ e, z, k))


def other_core():
    return route(lambda x, y, z, k: (x, y, z, k ^ 1))


def send(x, pairs):
    return lax.ppermute(x, AXES, pairs)


BF16 = jnp.bfloat16
F32 = jnp.float32
NT = (((1,), (1,)), ((), ()))
TN = (((0,), (0,)), ((), ()))
VMEM_LIMIT = 16 * 1024 * 1024
FIRST_LIMIT = 56 * 1024 * 1024
TAIL = 16
BLOCK = 256
SHIFT = 34.0
LOWEST = -60.0


def dot(a, b, dims=(((1,), (0,)), ((), ()))):
    return lax.dot_general(a, b, dims, preferred_element_type=F32)


def call(kernel, out_shape, args, flops=0, scratch=(), hbm=0, limit=VMEM_LIMIT):
    size = sum(a.size * a.dtype.itemsize for a in args)
    size += sum(math.prod(o.shape) * o.dtype.itemsize for o in jax.tree.leaves(out_shape))
    size = size if flops else 0
    return pl.pallas_call(
        kernel,
        out_shape=out_shape,
        in_specs=(
            [pl.BlockSpec(memory_space=pltpu.HBM)] * max(hbm, 0)
            + [pl.BlockSpec(memory_space=pltpu.VMEM)] * (len(args) - abs(hbm))
            + [pl.BlockSpec(memory_space=pl.ANY)] * max(-hbm, 0)
        ),
        out_specs=jax.tree.map(
            lambda o: pl.BlockSpec(memory_space=pltpu.SMEM if o.shape == (1, 1) else pltpu.VMEM), out_shape
        ),
        scratch_shapes=scratch,
        compiler_params=pltpu.CompilerParams(vmem_limit_bytes=limit),
        cost_estimate=pl.CostEstimate(flops=flops, bytes_accessed=size, transcendentals=0),
    )(*args)


def unit_rows(x):
    x32 = x.astype(F32)
    norms = jnp.sqrt(jnp.sum(x32 * x32, axis=-1, keepdims=True) + 1e-06)
    return (x32 / norms, norms)


def unit_block(student, teacher, sketch, out_ref):
    width = student.shape[1]
    out_ref[:, :width] = unit_rows(student)[0].astype(BF16)
    out_ref[:, width:] = unit_rows(dot(teacher, sketch))[0].astype(BF16)


def prepare_first_kernel(student_hbm, teacher_hbm, sketch_hbm, out_ref, *refs):
    *buffers, sems = refs
    copies = [
        pltpu.make_async_copy(src, dst, sems.at[n])
        for n, (src, dst) in enumerate(zip((student_hbm, teacher_hbm, sketch_hbm), buffers))
    ]
    for copy in copies:
        copy.start()
    for copy in copies:
        copy.wait()
    unit_block(*(ref[...] for ref in buffers), out_ref)


def prepare_kernel(student_ref, teacher_ref, sketch_ref, *refs):
    out_ref = refs[-1]
    unit_block(student_ref[...], teacher_ref[...], sketch_ref[...], out_ref)


def prepare(student, teacher, sketch, first_kernel, after=()):
    rows, width = student.shape
    out = jax.ShapeDtypeStruct((rows, 2 * width), BF16)
    args = (student, teacher, sketch)
    flops = 2 * rows * sketch.size
    if not first_kernel:
        return call(prepare_kernel, out, (*args, *after), flops, hbm=-len(after))
    scratch = [pltpu.VMEM(x.shape, x.dtype) for x in args] + [pltpu.SemaphoreType.DMA((len(args),))]
    return call(prepare_first_kernel, out, args, flops, scratch, hbm=3, limit=FIRST_LIMIT)


def lay_end_kernel(count, sizes, *refs):
    blocks = iter(refs[:count])
    for size, out_ref in zip(sizes, refs[count:]):
        at = 0
        for ref in (next(blocks) for _ in range(size)):
            out_ref[at : at + ref.shape[0], :] = ref[...]
            at += ref.shape[0]


def lay_end(groups, after=()):
    width = groups[0][0].shape[1]
    out = [jax.ShapeDtypeStruct((sum(block.shape[0] for block in group), width), BF16) for group in groups]
    args = [block for group in groups for block in group] + list(after)
    sizes = [len(group) for group in groups]
    return call(lambda *refs: lay_end_kernel(len(args), sizes, *refs), out, args, hbm=-len(after))


def products(img, txt_refs):
    width = img.shape[1] // 2
    p = [dot(img[:, width:], ref[:, width:], NT) for ref in txt_refs]
    q = [dot(img[:, :width], ref[:, :width], NT) for ref in txt_refs]
    return jnp.concatenate(p, axis=1), jnp.concatenate(q, axis=1)


def logits(img, txt_refs):
    p, q = products(img, txt_refs)
    return units * p, units * q


def load_block(n, own_ref, other_ref, block_ref):
    half = own_ref.shape[0] // BLOCK

    @pl.when(n < half)
    def _():
        block_ref[...] = own_ref[pl.ds(pl.multiple_of(n * BLOCK, BLOCK), BLOCK), :]

    @pl.when(n >= half)
    def _():
        block_ref[...] = other_ref[pl.ds(pl.multiple_of((n - half) * BLOCK, BLOCK), BLOCK), :]


def put_rows(row_ref, n, first, second, third):
    lane = lax.broadcasted_iota(jnp.int32, (BLOCK, 128), 1)
    packed = jnp.where(lane == 0, first, jnp.where(lane == 1, second, third))
    for k in range(BLOCK // 128):
        at = pl.multiple_of(n * BLOCK + k * 128, 128)
        row_ref[:, pl.ds(at, 128)] = packed[k * 128 : (k + 1) * 128].T[:8]


def put_sums(row_ref, n, *tiles):
    for k in range(BLOCK // 128):
        sums = [jnp.sum(tile[k * 128 : (k + 1) * 128].T, axis=0, keepdims=True) for tile in tiles]
        at = pl.multiple_of(n * BLOCK + k * 128, 128)
        row_ref[:, pl.ds(at, 128)] = stack_rows(*sums, (8, 128))


def stack_rows(first, second, third, shape):
    sub = lax.broadcasted_iota(jnp.int32, shape, 0)
    return jnp.where(sub == 0, first, jnp.where(sub == 1, second, third))


def merge_rows(new, old):
    top = jnp.maximum(new, old)
    new_w, old_w = jnp.exp2(new - top), jnp.exp2(old - top)
    total = new_w + old_w
    mean = (new_w[0:1] * new + old_w[0:1] * old) / total[0:1]
    lse = top + jnp.log2(total)
    return stack_rows(lse, lse, mean, new.shape)


def stats_kernel(pairs, has_old, own_ref, other_ref, *refs):
    halves, refs = refs[: 2 * pairs], refs[2 * pairs :]
    old_ref = refs[0] if has_old else None
    row_ref, col_ref, *tile_refs, block_ref, low_ref, high_ref, part_ref = refs[int(has_old) :]
    columns = col_ref.shape[1] // pairs
    blocks = 2 * own_ref.shape[0] // BLOCK

    def step(n, state):
        load_block(n, own_ref, other_ref, block_ref)
        row_sums, out = None, []
        for m in range(pairs):
            p, q = products(block_ref[...], halves[2 * m : 2 * m + 2])
            ep = jnp.exp2(units * p - SHIFT)
            eq = jnp.exp2(units * q - SHIFT)
            tiles = (ep, eq, ep * (p - q))
            span = pl.ds(pl.multiple_of(n * BLOCK, BLOCK), BLOCK)
            for k in range(4):
                at = k // 2 * (columns // 2)
                tile_refs[4 * m + k][span, :] = tiles[k % 2][:, at : at + columns // 2]
            out += [s + jnp.sum(x, axis=0, keepdims=True) for s, x in zip(state[3 * m : 3 * m + 3], tiles)]
            part = [sum(x[:, c : c + 128] for c in range(0, columns, 128)) for x in tiles]
            row_sums = part if row_sums is None else [x + y for x, y in zip(row_sums, part)]
        put_sums(row_ref, n, *row_sums)
        return tuple(out)

    zero = jnp.zeros((1, columns), F32)
    state = lax.fori_loop(0, blocks, step, (zero,) * (3 * pairs), unroll=pairs == 1)
    rows = row_ref[...]
    lowest = jnp.min(rows[0:2, :])
    for m in range(pairs):
        sp, sq, u = state[3 * m : 3 * m + 3]
        lowest = jnp.minimum(lowest, jnp.min(jnp.minimum(sp, sq)))
        col_ref[:, m * columns : (m + 1) * columns] = stack_rows(
            SHIFT + jnp.log2(sp), SHIFT + jnp.log2(sq), units * u / sp, (8, columns)
        )
    row_ref[...] = stack_rows(SHIFT + jnp.log2(rows), SHIFT + jnp.log2(rows), units * rows / rows[0:1], rows.shape)

    @pl.when(lowest < 2.0 ** (LOWEST - SHIFT))
    def _():
        def pair(m, _):
            for n in range(pairs):

                @pl.when(m == n)
                def _():
                    low_ref[...] = halves[2 * n][...]
                    high_ref[...] = halves[2 * n + 1][...]

            col = careful_stats(own_ref, other_ref, (low_ref, high_ref), part_ref, columns, block_ref)
            col_ref[:, pl.ds(pl.multiple_of(m * columns, columns), columns)] = col

            @pl.when(m == 0)
            def _():
                row_ref[...] = part_ref[...]

            @pl.when(m > 0)
            def _():
                row_ref[...] = merge_rows(part_ref[...], row_ref[...])

            return 0

        lax.fori_loop(0, pairs, pair, 0)

    if has_old:
        row_ref[...] = merge_rows(row_ref[...], old_ref[...])


def careful_stats(own_ref, other_ref, txt_refs, row_ref, columns, block_ref):

    def step(n, state):
        load_block(n, own_ref, other_ref, block_ref)
        p, q = logits(block_ref[...], txt_refs)
        d = p - q
        mp = jnp.max(p, axis=1, keepdims=True)
        mq = jnp.max(q, axis=1, keepdims=True)
        e = jnp.exp2(p - mp)
        sp = jnp.sum(e, axis=1, keepdims=True)
        u = jnp.sum(e * d, axis=1, keepdims=True)
        sq = jnp.sum(jnp.exp2(q - mq), axis=1, keepdims=True)
        put_rows(row_ref, n, mp + jnp.log2(sp), mq + jnp.log2(sq), u / sp)
        mp = jnp.maximum(jnp.max(p, axis=0, keepdims=True), state[0])
        mq = jnp.maximum(jnp.max(q, axis=0, keepdims=True), state[3])
        e = jnp.exp2(p - mp)
        old = jnp.exp2(state[0] - mp)
        sp = jnp.sum(e, axis=0, keepdims=True) + old * state[1]
        u = jnp.sum(e * d, axis=0, keepdims=True) + old * state[2]
        sq = jnp.sum(jnp.exp2(q - mq), axis=0, keepdims=True) + jnp.exp2(state[3] - mq) * state[4]
        return (mp, sp, u, mq, sq)

    low = jnp.full((1, columns), -1e30, F32)
    zero = jnp.zeros((1, columns), F32)
    blocks = 2 * own_ref.shape[0] // BLOCK
    mp, sp, u, mq, sq = lax.fori_loop(0, blocks, step, (low, zero, zero, low, zero))
    return stack_rows(mp + jnp.log2(sp), mq + jnp.log2(sq), u / sp, (8, columns))


def tile_stats(own, other, halves, old):
    pairs = len(halves) // 2
    half = halves[0].shape
    columns = len(halves) * half[0]
    rows = 2 * own.shape[0]
    args = [own, other, *halves] + ([] if old is None else [old])
    tile = jax.ShapeDtypeStruct((rows, half[0]), F32)
    row, col, *tiles = call(
        lambda *refs: stats_kernel(pairs, old is not None, *refs),
        (jax.ShapeDtypeStruct((8, rows), F32), jax.ShapeDtypeStruct((8, columns), F32), *[tile] * (2 * len(halves))),
        args,
        2 * rows * columns * own.shape[1],
        scratch=[
            pltpu.VMEM((BLOCK, half[1]), BF16),
            pltpu.VMEM(half, BF16),
            pltpu.VMEM(half, BF16),
            pltpu.VMEM((8, rows), F32),
        ],
    )
    return row, col, [tiles[n : n + 2] for n in range(0, len(tiles), 2)]


def merge(parts):
    top = parts[0]
    for part in parts[1:]:
        top = jnp.maximum(top, part)
    weights = [jnp.exp2(part - top) for part in parts]
    total = sum(weights)
    mean = sum(pltpu.roll(w, 2, 0) * part for w, part in zip(weights, parts)) / pltpu.roll(total, 2, 0)
    sub = lax.broadcasted_iota(jnp.int32, top.shape, 0)
    return jnp.where((sub == 2) | (sub == 5), mean, top + jnp.log2(total))


def on_core(core):
    return pl.when(lax.rem(lax.axis_index("col"), CORES) == core)


def lanes(*index):
    at = 0
    for i in index:
        at = at * SIDE + i
    return slice(at * 128, (at + 1) * 128)


def rows_3(first, second):
    return jnp.concatenate([first[:3], second[:3], first[:2]], axis=0)


def local_kernel(row_ref, near_ref, far_ref, out_ref):
    def columns(second, first):
        if second == 2:
            return far_ref[:, lanes(first)]
        half, at = divmod(first, SIDE // 2)
        return near_ref[:, lanes({0: (0, 2), 1: (4, 8), 3: (6, 10)}[second][half] + at)]

    for core in range(CORES):

        @on_core(core)
        def _():
            for x in range(SIDE):
                for y in range(SIDE):
                    col = columns(y, x) if core == 0 else columns(x, y)
                    row = col
                    if x < CORES:
                        row = row_ref[:, lanes(x if core == 0 else 1 - x, y)]
                    out_ref[:, lanes(x, y)] = rows_3(col, row)


def chip_kernel(own_ref, got_ref, out_ref):
    @on_core(0)
    def _():
        out_ref[...] = rows_3(own_ref[...], got_ref[...])

    @on_core(1)
    def _():
        rows = merge([jnp.concatenate([r[3:6, :1024], r[3:6, :1024], r[:2, :1024]], axis=0) for r in (own_ref, got_ref)])
        out_ref[...] = jnp.zeros(out_ref.shape, F32)
        for z in range(SIDE):
            out_ref[:, lanes(z, 0)] = rows_3(rows[:, lanes(0, z)], rows[:, lanes(1, z)])


def line_kernel(own_ref, g1, g2, g3, out_ref):
    width = own_ref.shape[1] // SIDE
    got = (own_ref, g1, g2, g3)
    for n in range(SIDE):
        parts = [got[e][:, (n ^ e) * width : ((n ^ e) + 1) * width] for e in range(SIDE)]
        out_ref[:, n * width : (n + 1) * width] = merge(parts)


def split_kernel(own_ref, got_ref, col_ref, row_ref):
    for core in range(CORES):

        @on_core(core)
        def _():
            cols, rows = (own_ref, got_ref) if core == 0 else (got_ref, own_ref)
            col_ref[...] = rows_3(cols[3 * core :, :][:3], cols[3 * core :, :][:3])
            for k in range(CORES):
                first = 3 * (k ^ core)
                for z in range(SIDE):
                    part = rows[:, lanes(z, 0)][first : first + 3]
                    row_ref[:, lanes(k, z)] = rows_3(part, part)


def plane_kernel(own_ref, g1, g2, g3, row_ref, out_ref, row_tail_ref, col_tail_ref, lowest_ref):
    got = (own_ref, g1, g2, g3)
    for x in range(SIDE):
        for y in range(SIDE):
            part = merge([got[e][:, lanes(x, y ^ e)] for e in range(SIDE)])

            @on_core(0)
            def _():
                out_ref[:, lanes(y, x)] = part

            @on_core(1)
            def _():
                out_ref[:, lanes(x, y)] = part

    put_tail(row_tail_ref, 0, kl_sum(row_ref[...]))
    put_tail(col_tail_ref, 0, kl_sum(out_ref[...]))
    lowest = jnp.minimum(
        jnp.min(row_ref[0:2, :], axis=1, keepdims=True), jnp.min(out_ref[0:2, :], axis=1, keepdims=True)
    )
    lowest_ref[...] = jnp.broadcast_to(jnp.min(lowest, axis=0, keepdims=True), lowest_ref.shape)


def exchange(row, cols):
    columns = sum(col.shape[1] for col in cols)
    out = jax.ShapeDtypeStruct((8, columns), F32)
    tail = jax.ShapeDtypeStruct((TAIL, columns // SIDE), BF16)
    local = call(local_kernel, out, (row, *cols))
    chip = call(chip_kernel, out, (local, send(local, other_core())))
    line = call(line_kernel, out, (chip, *(send(chip, x_or_z(e)) for e in ORDER)))
    col, row = call(split_kernel, (out, jax.ShapeDtypeStruct(row.shape, F32)), (line, send(line, other_core())))
    parts = [send(col, along_y(e)) for e in ORDER]
    col, *rest = call(plane_kernel, (out, tail, tail, jax.ShapeDtypeStruct((8, 128), F32)), (col, *parts, row))
    return row, col, *rest


def kl_sum(stats):
    kl = stats[2:3, :] - (stats[0:1, :] - stats[1:2, :])
    return jnp.sum(kl, axis=1, keepdims=True)


def put_tail(ref, at, value):
    shape = (TAIL, ref.shape[1])
    rest = jnp.broadcast_to(value, shape)
    sub = lax.broadcasted_iota(jnp.int32, shape, 0)
    tail = jnp.zeros(shape, F32)
    for n in range(3):
        part = rest.astype(BF16).astype(F32)
        tail = jnp.where(sub == n, part, tail)
        rest = rest - part
    ref[at : at + TAIL, :] = tail.astype(BF16)


def get_tail(ref, at):
    return jnp.sum(ref[at : at + TAIL, :].astype(F32), axis=0, keepdims=True)


def grad_kernel(piece, own_ref, other_ref, low_ref, high_ref, row_ref, col_ref, lowest_ref, *refs):
    ep_low, eq_low, ep_high, eq_high, *tail, g_ref, out_ref, block_ref = refs
    txt_refs = (low_ref, high_ref)
    columns = g_ref.shape[1]
    width = own_ref.shape[1] // 2
    half = own_ref.shape[0]
    blocks = 2 * half // BLOCK
    stats = col_ref[:, piece * columns : (piece + 1) * columns]
    lowest = lowest_ref[0, 0]

    def turned(n, x):
        out = []
        for k in range(BLOCK // 128):
            at = pl.multiple_of(n * BLOCK + k * 128, 128)
            out.append(jnp.concatenate([x(row_ref[:, pl.ds(at, 128)])] * 16, axis=0).T)
        out = jnp.concatenate(out, axis=0)
        return out[:, 0:1], out[:, 1:2]

    @pl.when(lowest >= LOWEST)
    def _():
        col = jnp.exp2(SHIFT - 1.0 - stats)

        def step(n, _):
            span = pl.ds(pl.multiple_of(n * BLOCK, BLOCK), BLOCK)
            rp, rq = turned(n, lambda x: jnp.exp2(SHIFT - 1.0 - x))
            ep = jnp.concatenate([ep_low[span, :], ep_high[span, :]], axis=1)
            eq = jnp.concatenate([eq_low[span, :], eq_high[span, :]], axis=1)
            g = eq * (rq + col[1:2, :]) - ep * (rp + col[0:1, :])
            g_ref[span, :] = g.astype(BF16)
            return 0

        lax.fori_loop(0, blocks, step, 0, unroll=True)

    @pl.when(lowest < LOWEST)
    def _():
        cp = stats[0:1, :] + 1.0
        cq = stats[1:2, :] + 1.0

        def step(n, _):
            load_block(n, own_ref, other_ref, block_ref)
            rp, rq = turned(n, lambda x: x + 1.0)
            p, q = logits(block_ref[...], txt_refs)
            g = (jnp.exp2(q - rq) - jnp.exp2(p - rp)) + (jnp.exp2(q - cq) - jnp.exp2(p - cp))
            g_ref[pl.ds(pl.multiple_of(n * BLOCK, BLOCK), BLOCK), :] = g.astype(BF16)
            return 0

        lax.fori_loop(0, blocks, step, 0)

    total = dot(g_ref[:half, :], own_ref[:, :width], TN) + dot(g_ref[half:, :], other_ref[:, :width], TN)
    out_ref[:columns, :] = total.astype(out_ref.dtype)
    if tail:
        out_ref[columns:, :] = tail[0][...]


def tile_grad(own, other, txt, tiles, stats, piece):
    row, col, row_tail, _, lowest = stats
    rows = own.shape[0] + other.shape[0]
    columns, width = 2 * txt[0].shape[0], own.shape[1]
    shape = jax.ShapeDtypeStruct
    out = shape((columns + TAIL, width // 2), BF16) if piece else shape((columns, width // 2), F32)
    return call(
        lambda *refs: grad_kernel(piece, *refs),
        (shape((rows, columns), BF16), out),
        (own, other, *txt, row, col, lowest, *tiles) + ((row_tail,) if piece else ()),
        0,
        scratch=[pltpu.VMEM((BLOCK, width), BF16)],
    )


def image_rows(first, half, grad_refs, txt_refs, store):
    rows, width = txt_refs[0].shape
    width //= 2

    def step(n, _):
        at = pl.multiple_of(n * BLOCK, BLOCK)
        total = None
        for m, txt_ref in enumerate(txt_refs):
            at_column = m % 2 * rows
            part = dot(grad_refs[m // 2][pl.ds(first + at, BLOCK), at_column : at_column + rows], txt_ref[:, :width])
            total = part if total is None else total + part
        store(pl.ds(at, BLOCK), total)
        return 0

    lax.fori_loop(0, half // BLOCK, step, 0, unroll=True)


def other_images_kernel(*refs):
    tail_ref, out_ref = refs[3 * SIDE :]
    half = out_ref.shape[0] - TAIL

    def store(span, value):
        out_ref[span, :] = value.astype(BF16)

    image_rows(half, half, refs[:SIDE], refs[SIDE : 3 * SIDE], store)
    out_ref[half:, :] = tail_ref[...]


def own_images_kernel(*refs):
    out_ref = refs[-1]

    def store(span, value):
        out_ref[span, :] = value

    image_rows(0, out_ref.shape[0], refs[:SIDE], refs[SIDE : 3 * SIDE], store)


def image_grads(grads, txts, tail, after):
    rows, columns = grads[0].shape
    txts = [half for piece in txts for half in piece]
    width = txts[0].shape[1] // 2
    half = rows // 2
    shape = jax.ShapeDtypeStruct
    flops = 0
    message = call(other_images_kernel, shape((half + TAIL, width), BF16), (*grads, *txts, tail), flops)
    own = call(own_images_kernel, shape((half, width), F32), (*grads, *txts, *after), flops, hbm=-len(after))
    return message, own


def combine_kernel(count, own_ref, tail_ref, *refs):
    got, outs = refs[:count], refs[-SIDE:]
    size = own_ref.shape[0]
    step = size // SIDE
    value = get_tail(tail_ref, 0) + sum(get_tail(ref, size) for ref in got)
    for n, ref in enumerate(outs):
        span = slice(n * step, (n + 1) * step)
        total = own_ref[span, :]
        for part in got:
            total = total + part[span, :].astype(F32)
        ref[:step, :] = total.astype(ref.dtype)
        if n:
            put_tail(ref, step, value)
        else:
            ref[step:, :] = jnp.broadcast_to(value, (8, value.shape[1]))


def combine(own, tail, got, after=()):
    size, width = own.shape
    step = size // SIDE
    message = jax.ShapeDtypeStruct((step + TAIL, width), BF16)
    keep = jax.ShapeDtypeStruct((step + 8, width), F32)
    return call(
        lambda *refs: combine_kernel(len(got), *refs),
        (keep, message, message, message),
        (own, tail, *got, *after),
        hbm=-len(after),
    )


def tangent(x_ref, keep_ref, got, grad_ref):
    rows = x_ref.shape[0]
    u, n = unit_rows(x_ref[...])
    du = scale * (keep_ref[:rows, :] + sum(ref[:rows, :].astype(F32) for ref in got))
    grad_ref[...] = (du - u * jnp.sum(u * du, axis=-1, keepdims=True)) / n
    return keep_ref[rows : rows + 1, :] + sum(get_tail(ref, rows) for ref in got)


def finish_kernel(factor, *refs):
    *ins, grad_image_ref, grad_text_ref, loss_ref = refs
    each = len(ins) // 2
    value = jnp.zeros((1, grad_text_ref.shape[1]), F32)
    for n, grad_ref in enumerate((grad_image_ref, grad_text_ref)):
        x_ref, keep_ref, *got = ins[n * each : (n + 1) * each]
        value = value + tangent(x_ref, keep_ref, got, grad_ref)
    loss_ref[0, 0] = factor * jnp.max(value)


def finish(image, text, factor):
    loss = jax.ShapeDtypeStruct((1, 1), F32)
    out = tuple(jax.ShapeDtypeStruct(x.shape, F32) for x in (image[0], text[0])) + (loss,)
    return call(lambda *refs: finish_kernel(factor, *refs), out, (*image, *text))


def shards(image_student, text_student, image_teacher, text_teacher, sketch):
    rows, width = image_student.shape
    txt = prepare(text_student, text_teacher, sketch, True)

    blocks = [txt] + [send(txt, first(e)) for e in range(1, SIDE)]
    img = prepare(image_student, image_teacher, sketch, False, (blocks[1],))
    img_1, img_3 = send(img, along_z(1)), send(img, along_z(3))
    low, high = lay_end([blocks[:2], blocks[2:]], (img_1, img_3))
    low_1, low_3 = send(low, second(1)), send(low, second(3))
    high_1, high_3 = send(high, second(1)), send(high, second(3))
    low_2, high_2 = send(low_3, second(1)), send(high_1, second(3))
    txt_all = [(low, high), (low_1, high_1), (low_2, high_2), (low_3, high_3)]
    (own,) = lay_end([[img, img_1, send(img, along_z(2)), img_3]], (low_1, low_3, high_1, high_3))
    other = send(own, other_core())

    row, near_col, near = tile_stats(own, other, (low, high, low_1, low_3, high_1, high_3), None)
    row, far_col, far = tile_stats(own, other, (low_2, high_2), row)
    tiles = [near[0] + near[1], near[2] + near[4], far[0] + far[1], near[3] + near[5]]
    stats = exchange(row, (near_col, far_col))

    grads, got = [None] * SIDE, []
    for b in (3, 1, 2):
        grads[b], message = tile_grad(own, other, txt_all[b], tiles[b], stats, b)
        got.append(send(message, second(b)))
    grads[0], own_txt = tile_grad(own, other, txt_all[0], tiles[0], stats, 0)
    message, own_img = image_grads(grads, txt_all, stats[3], got[:2])
    keep, *messages = combine(own_img, stats[3], [send(message, other_core())])
    image = [image_student, keep] + [send(messages[e - 1], along_z(e)) for e in (3, 2, 1)]
    keep_txt, *messages_txt = combine(own_txt, stats[2], got, image[2:3])
    text = [text_student, keep_txt] + [send(messages_txt[e - 1], first(e)) for e in (2, 3, 1)]
    pairs = rows * lax.axis_size("row") * lax.axis_size("col")
    grad_image, grad_text, mean_loss = finish(image, text, 0.5 / (LOG2E * pairs))
    return (grad_image, grad_text, mean_loss.reshape(()))


def solution(mesh):
    return jax.shard_map(
        shards,
        mesh=mesh,
        in_specs=(
            P(("row", "col"), None),
            P(("col", "row"), None),
            P(("row", "col"), None),
            P(("col", "row"), None),
            P(),
        ),
        out_specs=(P(("row", "col"), None), P(("col", "row"), None), P()),
        check_vma=False,
    )
```
